32 devices in a mesh: dp: 16 (over z, x, core), tensor: 2 (over y).
Axes of the slice: x: 2, y: 2, z: 4, core: 2. Of those that a mesh axis runs over, the one named last changes fastest.
Arguments:
- tokens: bfloat16 [2, 8192, 1152], P(None, 'dp'), may hold values from -6 to 6
- image_starts: int32 [2, 16], P(None, 'dp'), may hold values from 0 to 256
- g_attn_in: float32 [1152], replicated, may hold values from 0.5 to 1.5
- w_query: bfloat16 [1152, 1024], P(None, 'tensor'), may hold values from -0.1875 to 0.1875
- w_key: bfloat16 [1152, 256], replicated, may hold values from -0.1875 to 0.1875
- w_value: bfloat16 [1152, 256], replicated, may hold values from -0.1875 to 0.1875
- g_query: float32 [256], replicated, may hold values from 0.25 to 1.75
- g_key: float32 [256], replicated, may hold values from 0.25 to 1.75
- w_out: bfloat16 [1024, 1152], P('tensor'), may hold values from -0.1875 to 0.1875
- g_attn_post: float32 [1152], replicated, may hold values from 0.5 to 1.5
- g_ffn_in: float32 [1152], replicated, may hold values from 0.5 to 1.5
- w_gate: bfloat16 [1152, 6912], P(None, 'tensor'), may hold values from -0.1875 to 0.1875
- w_up: bfloat16 [1152, 6912], P(None, 'tensor'), may hold values from -0.1875 to 0.1875
- w_down: bfloat16 [6912, 1152], P('tensor'), may hold values from -0.078125 to 0.078125
- g_ffn_post: float32 [1152], replicated, may hold values from 0.5 to 1.5
- cotangent: bfloat16 [2, 8192, 1152], P(None, 'dp'), may hold values from -6 to 6
Outputs:
- output: bfloat16 [2, 8192, 1152], P(None, 'dp')
- grad_input: float32 [2, 8192, 1152], P(None, 'dp')
- grad_g_attn_in: float32 [1152], P('dp')
- grad_w_query: float32 [1152, 1024], P('dp', 'tensor')
- grad_w_key: float32 [1152, 256], P('dp')
- grad_w_value: float32 [1152, 256], P('dp')
- grad_g_query: float32 [256], P('dp')
- grad_g_key: float32 [256], P('dp')
- grad_w_out: float32 [1024, 1152], P('tensor', 'dp')
- grad_g_attn_post: float32 [1152], P('dp')
- grad_g_ffn_in: float32 [1152], P('dp')
- grad_w_gate: float32 [1152, 6912], P('dp', 'tensor')
- grad_w_up: float32 [1152, 6912], P('dp', 'tensor')
- grad_w_down: float32 [6912, 1152], P('tensor', 'dp')
- grad_g_ffn_post: float32 [1152], P('dp')
The draws below stay inside these ranges and needn't reach their ends.
Inputs may be any that keep to these rules, and one draw needn't show every extreme that they name: `image_starts`: each aligned block of 512 tokens holds exactly one image span of 256 tokens, starting this many tokens into the block.
All inputs are finite; a program needn't handle non-finite values.
Results may differ from the reference program's by a relative error of at most 0.019.
Values may be sent and summed in bfloat16 or wider, within the bound.
No kernel may reach another device: no remote copies, remote signals or barrier semaphores. Data moves between devices by JAX's collectives and lax.ppermute only.
A program may use at most 384 MiB of HBM per device.

```python
import jax
import jax.numpy as jnp
from jax import lax

D = 1152
H = 4
HD = 256
FF = 6912
WINDOW = 512
IMG = 256
SEQ_LEN = 4096
MB = 2
TOKENS = 8192


def with_ends(drawn, key, low, high):
    index_at = [jax.random.randint(jax.random.fold_in(key, axis), (), 0, length) for axis, length in enumerate(drawn.shape)]
    main_axis = drawn.shape.index(max(drawn.shape))
    next_to = index_at[:main_axis] + [(index_at[main_axis] + 1) % drawn.shape[main_axis]] + index_at[main_axis + 1:]
    return drawn.at[tuple(index_at)].set(low).at[tuple(next_to)].set(high)


def spiked(drawn, rng, source, target, shards_of, factor):
    owner, partner = [(jnp.arange(drawn.shape[axis_at]) // (drawn.shape[axis_at] // shards_of)).reshape([-1 if axis == axis_at else 1 for axis in range(drawn.ndim)]) for axis_at in (source, target)]
    chosen = jax.random.permutation(rng, shards_of)[partner]
    strong = (owner == chosen) | (owner == (partner + shards_of // 2) % shards_of)
    return jnp.where(strong, factor * drawn, drawn)


def block_scale(rng, extent, split, least, largest):
    loudness, own = 1.0, jax.random.fold_in(rng, 6)
    for axis_at, parts in split:
        draws = jnp.exp(jax.random.uniform(jax.random.fold_in(own, axis_at), (parts,), jnp.float32, least / len(split), largest / len(split)))
        loudness = loudness * jnp.repeat(draws, extent[axis_at] // parts).reshape([-1 if axis == axis_at else 1 for axis in range(len(extent))])
    return loudness


def bell_draw(own_key, dims, spread, limit, shards=(), held_as=jnp.bfloat16):
    level = block_scale(own_key, dims, shards, -0.22, 0.18) if shards else 1.0
    values = jax.random.normal(own_key, dims, jnp.float32) * spread * level
    return jnp.minimum(jnp.maximum(values, -limit), limit).astype(held_as)


def heavy_noise(key, shape, width, bound, pieces, heavy, kind=jnp.bfloat16):
    values = width * jax.random.normal(key, shape, jnp.float32)
    if pieces:
        values = values * block_scale(key, shape, pieces, -0.22, 0.18)
    return jnp.clip(spiked(values, jax.random.fold_in(key, 3), *heavy), -bound, bound).astype(kind)


def setup_inputs(seed: int = 0) -> dict:
    keys = jax.random.split(jax.random.key(seed), 17)
    tokens = bell_draw(keys[0], (MB, TOKENS, D), 1.0, 6.0, ((1, 16),))
    image_starts = with_ends(jax.random.randint(keys[1], (MB, TOKENS // WINDOW), 0, WINDOW - IMG + 1), jax.random.fold_in(keys[1], 1), 0, WINDOW - IMG).astype(jnp.int32)
    g_attn_in = jnp.clip(1.0 + 0.1 * jax.random.normal(keys[2], (D,), jnp.float32), 0.5, 1.5)
    w_query = bell_draw(keys[3], (D, H * HD), D ** -0.5, 0.1875, ((1, 2),))
    w_key = bell_draw(keys[4], (D, HD), D ** -0.5, 0.1875)
    w_value = bell_draw(keys[5], (D, HD), D ** -0.5, 0.1875)
    g_query = jnp.clip(1.0 + 0.15 * jax.random.normal(keys[6], (HD,), jnp.float32), 0.25, 1.75)
    g_key = jnp.clip(1.0 + 0.15 * jax.random.normal(keys[7], (HD,), jnp.float32), 0.25, 1.75)
    w_out = bell_draw(keys[8], (H * HD, D), (H * HD) ** -0.5, 0.1875, ((0, 2),))
    g_attn_post = jnp.clip(1.0 + 0.1 * jax.random.normal(keys[9], (D,), jnp.float32), 0.5, 1.5)
    g_ffn_in = jnp.clip(1.0 + 0.1 * jax.random.normal(keys[10], (D,), jnp.float32), 0.5, 1.5)
    w_gate = bell_draw(keys[11], (D, FF), D ** -0.5, 0.1875, ((1, 2),))
    w_up = bell_draw(keys[12], (D, FF), D ** -0.5, 0.1875, ((1, 2),))
    w_down = bell_draw(keys[13], (FF, D), FF ** -0.5, 0.078125, ((0, 2),))
    g_ffn_post = jnp.clip(1.0 + 0.1 * jax.random.normal(keys[14], (D,), jnp.float32), 0.5, 1.5)
    cotangent = heavy_noise(keys[15], (MB, TOKENS, D), 1.0, 6.0, ((1, 16),), (1, 2, 16, 2.0))
    return {"tokens": tokens, "image_starts": image_starts, "g_attn_in": g_attn_in, "w_query": w_query, "w_key": w_key, "w_value": w_value, "g_query": g_query, "g_key": g_key, "w_out": w_out, "g_attn_post": g_attn_post, "g_ffn_in": g_ffn_in, "w_gate": w_gate, "w_up": w_up, "w_down": w_down, "g_ffn_post": g_ffn_post, "cotangent": cotangent}


EPSILON = 1e-06
HIGHEST = lax.Precision.HIGHEST
NEGATIVE = -1e+30

@jax.custom_vjp
def low(v):
    return lax.optimization_barrier(v.astype(jnp.bfloat16)).astype(jnp.float32)

@jax.custom_vjp
def low_back(v):
    return v

def low_keep(v):
    return (low(v), None)

def low_pass(kept, grad):
    return (grad,)

def back_keep(v):
    return (v, None)

def back_low(kept, grad):
    return (low(grad),)
low.defvjp(low_keep, low_pass)
low_back.defvjp(back_keep, back_low)

def norm_rows(values, gain):
    return values * lax.rsqrt(lax.optimization_barrier(jnp.mean(values * values, axis=-1, keepdims=True)) + EPSILON) * gain

def rotate(values, cosine, sine_table):
    half_width = values.shape[-1] // 2
    front_half = values[..., :half_width]
    back_half = values[..., half_width:]
    return jnp.concatenate([front_half * cosine - back_half * sine_table, back_half * cosine + front_half * sine_table], axis=-1)

def angle_tables(places):
    half_width = HD // 2
    frequency = 10000.0 ** (-2.0 * jnp.arange(half_width, dtype=jnp.float32) / HD)
    angles = places.astype(jnp.float32)[:, None] * frequency[None, :]
    return (jnp.cos(angles), jnp.sin(angles))

def in_span(offsets, row_count):
    relative = jnp.arange(row_count, dtype=jnp.int32) % WINDOW
    starts = jnp.repeat(offsets.astype(jnp.int32), WINDOW)
    return (relative >= starts) & (relative < starts + IMG)

def block_mask(query_local, key_local, span_query, span_key, seq_offset):
    causal = (key_local[None, :] <= query_local[:, None]) & (query_local[:, None] - key_local[None, :] < WINDOW)
    same_block = key_local[None, :] // WINDOW == query_local[:, None] // WINDOW
    image = span_query[:, None] & span_key[None, :] & same_block
    return (key_local[None, :] + seq_offset >= 0) & (causal | image)

def attend(query_all, key_all, value_all, span_all):
    length = query_all.shape[0]
    block_count = length // WINDOW
    key_pad = jnp.concatenate([jnp.zeros((WINDOW, HD), key_all.dtype), key_all], 0)
    value_pad = jnp.concatenate([jnp.zeros((WINDOW, HD), value_all.dtype), value_all], 0)
    span_pad = jnp.concatenate([jnp.zeros((WINDOW,), jnp.bool_), span_all], 0)

    def one_block(block_index):
        first_row = block_index * WINDOW
        query_block = lax.dynamic_slice_in_dim(query_all, first_row, WINDOW, 0)
        key_block = lax.dynamic_slice_in_dim(key_pad, first_row, 2 * WINDOW, 0)
        value_block = lax.dynamic_slice_in_dim(value_pad, first_row, 2 * WINDOW, 0)
        span_query = lax.dynamic_slice_in_dim(span_all, first_row, WINDOW, 0)
        span_key = lax.dynamic_slice_in_dim(span_pad, first_row, 2 * WINDOW, 0)
        query_local = first_row + jnp.arange(WINDOW, dtype=jnp.int32)
        key_local = first_row - WINDOW + jnp.arange(2 * WINDOW, dtype=jnp.int32)
        valid = block_mask(query_local, key_local, span_query, span_key, 0)
        scores = low_back(jnp.einsum('qhd,kd->hqk', query_block, key_block, precision=HIGHEST))
        scores = jnp.where(valid[None], scores, NEGATIVE)
        row_peak = lax.optimization_barrier(jnp.max(scores, axis=-1, keepdims=True))
        shifted = jnp.exp(scores - row_peak)
        probs_low = low(shifted / lax.optimization_barrier(jnp.sum(shifted, axis=-1, keepdims=True)))
        return jnp.einsum('hqk,kd->qhd', probs_low, value_block, precision=HIGHEST)
    blocks = lax.map(jax.checkpoint(one_block), jnp.arange(block_count, dtype=jnp.int32))
    return blocks.reshape(length, -1)

def layer_forward(row_values, offsets, g_attn_in, w_query, w_key, w_value, g_query, g_key, w_out, g_attn_post, g_ffn_in, w_gate, w_up, w_down, g_ffn_post):
    length = row_values.shape[0]
    cosine, sine_table = angle_tables(jnp.arange(length, dtype=jnp.int32))
    span_all = in_span(offsets, length)
    normed = low(norm_rows(row_values, g_attn_in))
    query_raw = low_back(jnp.dot(normed, w_query, precision=HIGHEST)).reshape(length, H, HD)
    key_raw = low_back(jnp.dot(normed, w_key, precision=HIGHEST))
    value_all = low(low_back(jnp.dot(normed, w_value, precision=HIGHEST)))
    query_all = low(rotate(norm_rows(query_raw, g_query), cosine[:, None, :], sine_table[:, None, :]) * HD ** (-0.5))
    key_all = low(rotate(norm_rows(key_raw, g_key), cosine, sine_table))
    mixed = low_back(low(attend(query_all, key_all, value_all, span_all)))
    branch = low_back(jnp.dot(mixed, w_out, precision=HIGHEST))
    middle = row_values + norm_rows(branch, g_attn_post)
    normed_ffn = low(norm_rows(middle, g_ffn_in))
    gate_all = low_back(jnp.dot(normed_ffn, w_gate, precision=HIGHEST))
    up_all = low_back(jnp.dot(normed_ffn, w_up, precision=HIGHEST))
    hidden = low(jax.nn.gelu(gate_all, approximate=True) * up_all)
    ffn_out = low_back(jnp.dot(hidden, w_down, precision=HIGHEST))
    return middle + norm_rows(ffn_out, g_ffn_post)

def reference(tokens, image_starts, g_attn_in, w_query, w_key, w_value, g_query, g_key, w_out, g_attn_post, g_ffn_in, w_gate, w_up, w_down, g_ffn_post, cotangent):
    weights = tuple((element.astype(jnp.float32) for element in (g_attn_in, w_query, w_key, w_value, g_query, g_key, w_out, g_attn_post, g_ffn_in, w_gate, w_up, w_down, g_ffn_post)))
    sequences = TOKENS // SEQ_LEN
    inputs = tokens.astype(jnp.float32).reshape(MB * sequences, SEQ_LEN, D)
    offsets = image_starts.reshape(MB * sequences, SEQ_LEN // WINDOW)

    def forward(values, *params):

        def per_sequence(element):
            return layer_forward(element[0], element[1], *params)
        return lax.map(jax.checkpoint(per_sequence), (values, offsets))
    result, pullback = jax.vjp(forward, inputs, *weights)
    gradients = pullback(cotangent.astype(jnp.float32).reshape(MB * sequences, SEQ_LEN, D))
    output = result.reshape(MB, TOKENS, D).astype(jnp.bfloat16)
    return (output, gradients[0].reshape(MB, TOKENS, D), gradients[1], gradients[2], gradients[3], gradients[4], gradients[5], gradients[6], gradients[7], gradients[8], gradients[9], gradients[10], gradients[11], gradients[12], gradients[13])
```

```python
import jax
import jax.numpy as jnp
from jax import lax
from jax.sharding import PartitionSpec as P

HD = 256
WINDOW = 512
IMG = 256
SEQ_LEN = 4096
EPSILON = 1e-06
NEGATIVE = -1e30
F32 = jnp.float32
BF16 = jnp.bfloat16


def dot(a, b, ca=1, cb=0):
    return lax.dot_general(a, b, (((ca,), (cb,)), ((), ())), preferred_element_type=F32)


def inv_rms(v):
    return lax.rsqrt(jnp.mean(v * v, axis=-1, keepdims=True) + EPSILON)


def pull_v(v, r, g, e):
    eg = e * g
    return r * eg - v * (r * r * r) * jnp.mean(v * eg, axis=-1, keepdims=True)


def rotate(v, cosine, sine):
    half = v.shape[-1] // 2
    a, b = v[..., :half], v[..., half:]
    return jnp.concatenate([a * cosine - b * sine, b * cosine + a * sine], axis=-1)


def angle_tables(places):
    half = HD // 2
    frequency = 10000.0 ** (-2.0 * jnp.arange(half, dtype=F32) / HD)
    angles = places.astype(F32)[:, None] * frequency[None, :]
    return jnp.cos(angles), jnp.sin(angles)


def swap_y(v):
    return lax.ppermute(v, "tensor", [(0, 1), (1, 0)])


def swap_dp(v, bit):
    n = lax.axis_size("dp")
    return lax.ppermute(v, "dp", [(i, i ^ (1 << bit)) for i in range(n)])


def shift_dp(v, steps):
    n = lax.axis_size("dp")
    first, last = max(0, -steps), min(n, n - steps)
    return lax.ppermute(v, "dp", [(i, i + steps) for i in range(first, last)])


def bits_of(n):
    return n.bit_length() - 1


def halves_first(a):
    n = lax.axis_size("dp")
    count = bits_of(n)
    t = a.T.reshape((2,) * count + (a.shape[1] // n, a.shape[0]))
    t = t.transpose(tuple(reversed(range(count))) + (count, count + 1))
    return t.reshape(2, a.shape[1] // 2, a.shape[0])


def my_bit(bit):
    return (lax.axis_index("dp") >> bit) & 1


def pick(a, i):
    return lax.dynamic_index_in_dim(a, i, 0, keepdims=False)


def scatter_sum(left, right):
    n = lax.axis_size("dp")
    mine = my_bit(0)
    got = swap_dp(dot(pick(left, 1 - mine), right).astype(BF16), 0)
    total = dot(pick(left, mine), right) + got.astype(F32)
    for bit in range(1, bits_of(n)):
        both = total.astype(BF16).reshape(2, total.shape[0] // 2, total.shape[1])
        mine = my_bit(bit)
        got = swap_dp(pick(both, 1 - mine), bit)
        total = pick(both, mine).astype(F32) + got.astype(F32)
    return total


def shards(
    tokens,
    image_starts,
    g_attn_in,
    w_query,
    w_key,
    w_value,
    g_query,
    g_key,
    w_out,
    g_attn_post,
    g_ffn_in,
    w_gate,
    w_up,
    w_down,
    g_ffn_post,
    cotangent,
):
    mb, rows, width = tokens.shape
    heads_own = w_query.shape[1] // HD
    heads = 2 * heads_own
    y = lax.axis_index("tensor")
    dp = lax.axis_index("dp")
    offset = dp % (SEQ_LEN // rows) * rows
    cosine, sine = angle_tables(offset + jnp.arange(rows, dtype=jnp.int32))
    cos_h, sin_h = cosine[:, None, :], sine[:, None, :]
    scale = HD ** -0.5

    core = my_bit(0)
    halfq = w_query.reshape(2, width // 2, -1)
    halfo = w_out.reshape(2, w_out.shape[0] // 2, width)

    def gather_other(two):
        part = swap_y(pick(two, core))
        other = swap_dp(part, 0)
        pair = jnp.stack([part, other])
        return jnp.concatenate([pick(pair, core), pick(pair, 1 - core)], 0)

    other_q = gather_other(halfq)
    other_o = gather_other(halfo)
    is0 = y == 0
    wq = jnp.where(
        is0,
        jnp.concatenate([w_query, other_q], 1),
        jnp.concatenate([other_q, w_query], 1),
    )
    wo = jnp.where(
        is0,
        jnp.concatenate([w_out, other_o], 0),
        jnp.concatenate([other_o, w_out], 0),
    )

    local = jnp.arange(rows, dtype=jnp.int32)
    window = jnp.arange(2 * rows, dtype=jnp.int32) - rows

    fw = []
    for m in range(mb):
        x = tokens[m].astype(F32)
        r0 = inv_rms(x)
        h1 = (x * r0 * g_attn_in).astype(BF16)
        key_raw = dot(h1, w_key)
        value = dot(h1, w_value).astype(BF16)
        rk = inv_rms(key_raw)
        key = rotate(key_raw * rk * g_key, cosine, sine).astype(BF16)
        near = shift_dp((key, value), 1)
        fw.append((x, r0, h1, key_raw, rk, key, value, near))

    at = []
    for m in range(mb):
        x, r0, h1, key_raw, rk, key, value, near = fw[m]
        query_raw = dot(h1, wq).reshape(rows, heads, HD)
        rq = inv_rms(query_raw)
        query = (rotate(query_raw * rq * g_query, cos_h, sin_h) * scale).astype(BF16)
        keys = jnp.concatenate([near[0], key], 0)
        values = jnp.concatenate([near[1], value], 0)
        start = image_starts[m, 0]
        in_q = (local >= start) & (local < start + IMG)
        in_k = (window >= start) & (window < start + IMG)
        back = local[:, None] - window[None, :]
        valid = ((back >= 0) & (back < WINDOW)) | (in_q[:, None] & in_k[None, :])
        valid = valid & (window[None, :] + offset >= 0)
        scores = jnp.einsum("qhd,kd->hqk", query, keys, preferred_element_type=F32)
        scores = jnp.where(valid[None], scores, NEGATIVE)
        peak = jnp.max(scores, axis=-1, keepdims=True)
        log_total = peak + jnp.log(jnp.sum(jnp.exp(scores - peak), axis=-1, keepdims=True))
        probs = jnp.exp(scores - log_total).astype(BF16)
        mixed = jnp.einsum("hqk,kd->qhd", probs, values, preferred_element_type=F32)
        mixed = mixed.reshape(rows, heads * HD).astype(BF16)
        branch = dot(mixed, wo)
        r1 = inv_rms(branch)
        middle = x + branch * r1 * g_attn_post
        r2 = inv_rms(middle)
        h2 = (middle * r2 * g_ffn_in).astype(BF16)
        at.append((query_raw, rq, query, keys, values, valid, log_total, mixed, branch, r1, middle, r2, h2))

    ff = []
    for m in range(mb):
        h2 = at[m][-1]
        gate = dot(h2, w_gate)
        up = dot(h2, w_up)
        hidden = (jax.nn.gelu(gate, approximate=True) * up).astype(BF16)
        part = dot(hidden, w_down).astype(BF16)
        ff.append((gate.astype(BF16), up.astype(BF16), hidden, part, swap_y(part)))

    outputs = []
    bw = []
    gain_post = 0.0
    for m in range(mb):
        gate, up, hidden, part, got = ff[m]
        middle = at[m][10]
        ffn = part.astype(F32) + got.astype(F32)
        r3 = inv_rms(ffn)
        cot = cotangent[m].astype(F32)
        outputs.append((middle + ffn * r3 * g_ffn_post).astype(BF16))
        d_ffn = pull_v(ffn, r3, g_ffn_post, cot).astype(BF16)
        gain_post = gain_post + jnp.sum(cot * ffn * r3, axis=0)
        d_hidden = dot(d_ffn, w_down, 1, 1)
        act, pull = jax.vjp(lambda v: jax.nn.gelu(v, approximate=True), gate.astype(F32))
        d_up = (d_hidden * act).astype(BF16)
        (d_gate,) = pull(d_hidden * up.astype(F32))
        d_gate = d_gate.astype(BF16)
        dh2 = (dot(d_gate, w_gate, 1, 1) + dot(d_up, w_up, 1, 1)).astype(BF16)
        bw.append((d_ffn, d_gate, d_up, dh2, swap_y(dh2), cot))

    def rows_of(parts):
        return jnp.concatenate(parts, 0)

    grad_down = scatter_sum(halves_first(rows_of([b[0] for b in bw])), rows_of([f[2] for f in ff]))
    h2_t = halves_first(rows_of([a[-1] for a in at]))
    grad_gate = scatter_sum(h2_t, rows_of([b[1] for b in bw]))
    grad_up = scatter_sum(h2_t, rows_of([b[2] for b in bw]))

    gain_ffn_in = gain_attn_post = gain_query = 0.0
    d_branches = []
    dqs = []
    back = []
    for m in range(mb):
        query_raw, rq, query, keys, values, valid, log_total, mixed, branch, r1, middle, r2, h2 = at[m]
        dh2_sum = bw[m][3].astype(F32) + bw[m][4].astype(F32)
        d_middle = bw[m][5] + pull_v(middle, r2, g_ffn_in, dh2_sum)
        gain_ffn_in = gain_ffn_in + jnp.sum(dh2_sum * middle * r2, axis=0)
        gain_attn_post = gain_attn_post + jnp.sum(d_middle * branch * r1, axis=0)
        d_branch = pull_v(branch, r1, g_attn_post, d_middle).astype(BF16)
        d_mixed = dot(d_branch, wo, 1, 1).astype(BF16).reshape(rows, heads, HD)
        scores = jnp.einsum("qhd,kd->hqk", query, keys, preferred_element_type=F32)
        scores = jnp.where(valid[None], scores, NEGATIVE)
        probs = jnp.exp(scores - log_total)
        d_probs = jnp.einsum("qhd,kd->hqk", d_mixed, values, preferred_element_type=F32)
        row_dot = jnp.sum(probs * d_probs, axis=-1, keepdims=True)
        d_scores = (probs * (d_probs - row_dot)).astype(BF16)
        d_query = jnp.einsum("hqk,kd->qhd", d_scores, keys, preferred_element_type=F32)
        d_key = jnp.einsum("hqk,qhd->kd", d_scores, query, preferred_element_type=F32)
        d_value = jnp.einsum("hqk,qhd->kd", probs.astype(BF16), d_mixed, preferred_element_type=F32)
        sent = shift_dp((d_key[:rows].astype(BF16), d_value[:rows].astype(BF16)), -1)
        e_q = rotate(d_query * scale, cos_h, -sin_h)
        gain_query = gain_query + jnp.sum(e_q * query_raw * rq, axis=(0, 1))
        dqr = pull_v(query_raw, rq, g_query, e_q).astype(BF16).reshape(rows, heads * HD)
        d_branches.append(d_branch)
        dqs.append(dqr)
        back.append((d_middle, d_key[rows:], d_value[rows:], sent))

    gain_key = gain_in = 0.0
    kvs = []
    grad_inputs = []
    for m in range(mb):
        x, r0, h1, key_raw, rk, key, value, near = fw[m]
        d_middle, d_key, d_value, sent = back[m]
        e_k = rotate(d_key + sent[0].astype(F32), cosine, -sine)
        gain_key = gain_key + jnp.sum(e_k * key_raw * rk, axis=0)
        dkr = pull_v(key_raw, rk, g_key, e_k).astype(BF16)
        dvr = (d_value + sent[1].astype(F32)).astype(BF16)
        d_h1 = dot(dqs[m], wq, 1, 1) + dot(dkr, w_key, 1, 1) + dot(dvr, w_value, 1, 1)
        gain_in = gain_in + jnp.sum(d_h1 * x * r0, axis=0)
        grad_inputs.append(d_middle + pull_v(x, r0, g_attn_in, d_h1))
        kvs.append(jnp.concatenate([dkr, dvr], 1))

    def own(a):
        return lax.dynamic_slice_in_dim(a, y * heads_own * HD, heads_own * HD, 1)

    grad_out = scatter_sum(halves_first(rows_of(d_branches)), own(rows_of([a[7] for a in at])))
    h1_t = halves_first(rows_of([f[2] for f in fw]))
    grad_qkv = scatter_sum(
        h1_t, jnp.concatenate([own(rows_of(dqs)), rows_of(kvs)], 1)
    )
    qw = heads_own * HD
    n = lax.axis_size("dp")
    wide = jnp.stack([gain_in, gain_post, gain_ffn_in, gain_attn_post])
    wide = wide.reshape(4, n, -1).transpose(1, 0, 2).reshape(n, -1)
    small = jnp.stack([gain_query, gain_key]).reshape(2, n, -1).transpose(1, 0, 2).reshape(n, -1)
    gains = lax.psum(jnp.concatenate([wide, small], 1), "dp")
    gains = pick(gains, dp)
    rps = width // n
    hps = HD // n
    g_in, g_post, g_ffn, g_attn = [gains[i * rps : (i + 1) * rps] for i in range(4)]
    gq = gains[4 * rps : 4 * rps + hps]
    gk = gains[4 * rps + hps :]
    return (
        jnp.stack(outputs),
        jnp.stack(grad_inputs),
        g_in,
        grad_qkv[:, :qw],
        grad_qkv[:, qw : qw + HD],
        grad_qkv[:, qw + HD :],
        gq,
        gk,
        grad_out.T,
        g_attn,
        g_ffn,
        grad_gate,
        grad_up,
        grad_down.T,
        g_post,
    )


def solution(mesh):
    rows = P(None, "dp", None)
    in_specs = (
        rows,
        P(None, "dp"),
        P(),
        P(None, "tensor"),
        P(),
        P(),
        P(),
        P(),
        P("tensor", None),
        P(),
        P(),
        P(None, "tensor"),
        P(None, "tensor"),
        P("tensor", None),
        P(),
        rows,
    )
    out_specs = (
        rows,
        rows,
        P("dp"),
        P("dp", "tensor"),
        P("dp", None),
        P("dp", None),
        P("dp"),
        P("dp"),
        P("tensor", "dp"),
        P("dp"),
        P("dp"),
        P("dp", "tensor"),
        P("dp", "tensor"),
        P("tensor", "dp"),
        P("dp"),
    )
    return jax.shard_map(shards, mesh=mesh, in_specs=in_specs, out_specs=out_specs, check_vma=False)
```

```python
import jax
import jax.numpy as jnp
from jax import lax
from jax.experimental import pallas as pl
from jax.experimental.pallas import tpu as pltpu
from jax.sharding import PartitionSpec as P
import numpy as np

HD = 256
WINDOW = 512
IMG = 256
SEQ_LEN = 4096
EPSILON = 1e-06
NEGATIVE = -1e30
SCALE = HD ** -0.5
GELU_C = 0.7978845608028654
GELU_A = 0.044715
F32 = jnp.float32
BF16 = jnp.bfloat16
VMEM_BYTES = 60 * 2**20
ATTN_IN, ATTN_POST, FFN_IN, FFN_POST = range(4)
QUERY, KEY = range(2)


def nn(a, b):
    return jnp.dot(a, b, preferred_element_type=F32)


def nt(a, b):
    return lax.dot_general(a, b, (((1,), (1,)), ((), ())), preferred_element_type=F32)


def inv_rms(v):
    return lax.rsqrt(jnp.mean(v * v, axis=-1, keepdims=True) + EPSILON)


def pull_v(v, r, g, e):
    eg = e * g
    return r * eg - v * (r * r * r * jnp.mean(v * eg, axis=-1, keepdims=True))


def rotate(v, cosine, sine):
    half = v.shape[-1] // 2
    a, b = v[:, :half], v[:, half:]
    return jnp.concatenate([a * cosine - b * sine, b * cosine + a * sine], axis=-1)


def rotate_back(v, cosine, sine):
    half = v.shape[-1] // 2
    a, b = v[:, :half], v[:, half:]
    return jnp.concatenate([a * cosine + b * sine, b * cosine - a * sine], axis=-1)


def angle_tables(places):
    half = HD // 2
    frequency = (10000.0 ** (-2.0 * np.arange(half) / HD)).astype(np.float32)
    angles = places.astype(F32)[:, None] * frequency[None, :]
    return jnp.cos(angles), jnp.sin(angles)


def swap_y(v):
    return lax.ppermute(v, "tensor", [(0, 1), (1, 0)])


def swap_dp(v, bit):
    n = lax.axis_size("dp")
    return lax.ppermute(v, "dp", [(i, i ^ (1 << bit)) for i in range(n)])


def shift_dp(v, steps):
    n = lax.axis_size("dp")
    first, last = max(0, -steps), min(n, n - steps)
    return lax.ppermute(v, "dp", [(i, i + steps) for i in range(first, last)])


def my_bit(bit):
    return (lax.axis_index("dp") >> bit) & 1


def after(value, *earlier):
    return lax.optimization_barrier((value,) + earlier)[0]


def pick(a, i):
    return lax.dynamic_index_in_dim(a, i, 0, keepdims=False)


class Chain:
    def __init__(self):
        self.last = ()
        self.first = []
        self.received = []

    def before_next(self, *arrays):
        self.first.extend(arrays)

    def moved(self, array):
        self.received.append(array)
        return array

    def take(self):
        taken, self.first = list(self.last) + self.first, []
        return taken


def call(body, grid, ins, outs, scratch, chain, scalars, *args, into=None, ahead=()):
    count = len(ins)
    ahead = list(ahead)
    skip = len(ahead)
    into = into or {}
    given = list(into.values())
    extra = given + [a for a in chain.take() if not any(a is g for g in given)]
    aliases = {1 + skip + count + k: out for k, out in enumerate(into)}

    anywhere = pl.BlockSpec(memory_space=pl.ANY)

    def inner(sc, *refs):
        body(sc, *refs[skip:skip + count], *refs[skip + count + len(extra):])

    results = pl.pallas_call(
        inner,
        grid_spec=pltpu.PrefetchScalarGridSpec(
            num_scalar_prefetch=1,
            grid=grid,
            in_specs=[anywhere] * skip + list(ins) + [anywhere] * len(extra),
            out_specs=[o[2] for o in outs],
            scratch_shapes=scratch,
        ),
        out_shape=[jax.ShapeDtypeStruct(s, d) for s, d, _ in outs],
        input_output_aliases=aliases,
        compiler_params=pltpu.CompilerParams(
            vmem_limit_bytes=VMEM_BYTES,
            dimension_semantics=("arbitrary",) * len(grid),
        ),
        cost_estimate=pl.CostEstimate(flops=10**14, bytes_accessed=1000, transcendentals=0),
    )(scalars, *ahead, *args, *extra)
    chain.last = (min(results, key=lambda r: r.size),)
    return results


def begin(prior, *sums):
    for k, s in enumerate(sums):
        s[...] = prior[k][...] if prior else jnp.zeros_like(s)


def one(ref, k):
    return ref[k:k + 1, :]


def whole(a):
    nd = len(a.shape)
    return pl.BlockSpec(a.shape, lambda *i: (0,) * nd)


def in_order(sc, at, own, other):
    first = sc[at] == 0
    return jnp.where(first, own, other), jnp.where(first, other, own)


def joined(sc, part, sibling):
    first = sc[1] == 0
    return jnp.concatenate([jnp.where(first, part, sibling), jnp.where(first, sibling, part)], 0)


def pre_attention(chain, scalars, x, gain, wk, wv, g_key, cosine, sine, step):
    total, width = x.shape
    rows = cosine.shape[0]

    def body(sc, x_ref, g_ref, wk_ref, wv_ref, gk_ref, cos_ref, sin_ref, h_ref, raw_ref, kv_ref):
        v = x_ref[...].astype(F32)
        h = (v * inv_rms(v) * one(g_ref, ATTN_IN)).astype(BF16)
        h_ref[...] = h
        raw = nn(h, wk_ref[...])
        raw_ref[...] = raw
        key = rotate(raw * inv_rms(raw) * one(gk_ref, KEY), cos_ref[...], sin_ref[...])
        kv_ref[:, :HD] = key.astype(BF16)
        kv_ref[:, HD:] = nn(h, wv_ref[...]).astype(BF16)

    per = rows // step
    table = pl.BlockSpec((step, HD // 2), lambda i, s: (i % per, 0))
    wide = pl.BlockSpec((step, width), lambda i, s: (i, 0))
    head = pl.BlockSpec((step, HD), lambda i, s: (i, 0))
    return call(
        body,
        (total // step,),
        [wide, whole(gain), whole(wk), whole(wv), whole(g_key), table, table],
        [
            ((total, width), BF16, wide),
            ((total, HD), F32, head),
            ((total, 2 * HD), BF16, pl.BlockSpec((step, 2 * HD), lambda i, s: (i, 0))),
        ],
        [],
        chain,
        scalars,
        x, gain, wk, wv, g_key, cosine, sine,
    )


def set_bias(sc, m, near_ref, own_ref, transposed):
    rows = near_ref.shape[0]
    q_dim, k_dim = (1, 0) if transposed else (0, 1)
    q = lax.broadcasted_iota(jnp.int32, (rows, rows), q_dim)
    k = lax.broadcasted_iota(jnp.int32, (rows, rows), k_dim)
    start = sc[2 + m]
    after = (k > q) & (sc[0] > 0)
    near_ref[...] = jnp.where(after, 0.0, NEGATIVE)
    in_q = (q >= start) & (q < start + IMG)
    in_k = (k >= start) & (k < start + IMG)
    own_ref[...] = jnp.where((k <= q) | (in_q & in_k), 0.0, NEGATIVE)


def queries(chain, scalars, at, h1, own, other, gains, cosine, sine, step, into):
    total, width = h1.shape
    columns = own.shape[1]
    weights = [own] if other is None else list(other)

    def body(sc, h_ref, *refs):
        w_refs = refs[:len(weights)]
        g_ref, cos_ref, sin_ref, raw_ref, q_ref = refs[len(weights):]
        w = w_refs[0][...] if other is None else joined(sc, w_refs[0][...], w_refs[1][...])
        both = nn(h_ref[...], w)
        raw_ref[...] = both.astype(BF16)
        for k in range(columns // HD):
            raw = both[:, k * HD:(k + 1) * HD]
            q = rotate(raw * inv_rms(raw) * one(g_ref, QUERY), cos_ref[...], sin_ref[...]) * SCALE
            q_ref[:, k * HD:(k + 1) * HD] = q.astype(BF16)

    per = cosine.shape[0] // step
    table = pl.BlockSpec((step, HD // 2), lambda i, s: (i % per, 0))
    out = pl.BlockSpec((step, columns), lambda i, s: (i, s[at] if other is None else 1 - s[at]))
    shape = (total, 2 * columns)
    return call(
        body,
        (total // step,),
        [pl.BlockSpec((step, width), lambda i, s: (i, 0))] + [whole(w) for w in weights]
        + [whole(gains), table, table],
        [(shape, BF16, out)] * 2,
        [],
        chain,
        scalars,
        h1, *weights, gains, cosine, sine,
        into={} if into is None else {0: into[0], 1: into[1]},
    )


def attention(chain, scalars, query, near, kv, rows):
    total = query.shape[0]
    heads = query.shape[1] // HD

    def body(sc, q_ref, nk_ref, k_ref, nv_ref, v_ref, mix_ref, near_bias, own_bias):
        @pl.when(pl.program_id(1) == 0)
        def _():
            set_bias(sc, pl.program_id(0), near_bias, own_bias, False)

        q = q_ref[...]
        near = jnp.exp(nt(q, nk_ref[...]) + near_bias[...])
        own = jnp.exp(nt(q, k_ref[...]) + own_bias[...])
        sums = jnp.sum(near, axis=-1, keepdims=True) + jnp.sum(own, axis=-1, keepdims=True)
        mix = nn(near.astype(BF16), nv_ref[...]) + nn(own.astype(BF16), v_ref[...])
        mix_ref[...] = (mix / sums).astype(BF16)

    key_at = pl.BlockSpec((rows, HD), lambda m, h, s: (m, 0))
    value_at = pl.BlockSpec((rows, HD), lambda m, h, s: (m, 1))
    out = pl.BlockSpec((rows, HD), lambda m, h, s: (m, h))
    return call(
        body,
        (total // rows, heads),
        [out, key_at, key_at, value_at, value_at],
        [(query.shape, BF16, out)],
        [pltpu.VMEM((rows, rows), F32)] * 2,
        chain,
        scalars,
        query, near, kv, near, kv,
    )[0]


def post_attention(chain, scalars, tensor_at, x, mixed, own, part, sibling, gains, step):
    total, width = x.shape

    def body(sc, x_ref, m_ref, own_ref, part_ref, sib_ref, g_ref, br_ref, mid_ref, h_ref):
        other = joined(sc, part_ref[...], sib_ref[...])
        first, second = in_order(sc, tensor_at, own_ref[...], other)
        branch = nn(m_ref[:, :half], first) + nn(m_ref[:, half:], second)
        br_ref[...] = branch.astype(BF16)
        middle = x_ref[...].astype(F32) + branch * inv_rms(branch) * one(g_ref, ATTN_POST)
        mid_ref[...] = middle
        h_ref[...] = (middle * inv_rms(middle) * one(g_ref, FFN_IN)).astype(BF16)

    half = own.shape[0]
    wide = pl.BlockSpec((step, width), lambda i, s: (i, 0))
    shape = (total, width)
    return call(
        body,
        (total // step,),
        [wide, pl.BlockSpec((step, mixed.shape[1]), lambda i, s: (i, 0)), whole(own), whole(part), whole(sibling), whole(gains)],
        [(shape, BF16, wide), (shape, F32, wide), (shape, BF16, wide)],
        [],
        chain,
        scalars,
        x, mixed, own, part, sibling, gains,
    )


def ffn_forward(chain, scalars, m, h2, wg, wu, wd, rows, tile, chunk):
    width, hidden = wg.shape
    steps = hidden // tile

    def body(sc, h_ref, wg_ref, wu_ref, wd_ref, act_ref, dact_ref, hid_ref, out_ref, acc):
        @pl.when(pl.program_id(0) == 0)
        def _():
            acc[...] = jnp.zeros_like(acc)

        w = jnp.concatenate([wg_ref[...], wu_ref[...]], 1)
        for r in range(rows // chunk):
            at = pl.ds(r * chunk, chunk)
            both = nn(h_ref[at, :], w)
            g, u = both[:, :tile], both[:, tile:]
            g2 = g * g
            t = jnp.tanh(g * (GELU_C + GELU_C * GELU_A * g2))
            half = 0.5 + 0.5 * t
            act = g * half
            dact = half + 0.5 * g * (1.0 - t * t) * (GELU_C + 3.0 * GELU_C * GELU_A * g2)
            act_ref[at, :] = act.astype(BF16)
            dact_ref[at, :] = (dact * u).astype(BF16)
            hid = (act * u).astype(BF16)
            hid_ref[at, :] = hid
            acc[at, :] += nn(hid, wd_ref[...])

        @pl.when(pl.program_id(0) == steps - 1)
        def _():
            out_ref[...] = acc[...].astype(BF16)

    col = pl.BlockSpec((width, tile), lambda i, s: (0, i))
    act = pl.BlockSpec((rows, tile), lambda i, s: (0, i))
    return call(
        body,
        (steps,),
        [pl.BlockSpec((rows, width), lambda i, s: (m, 0)), col, col, pl.BlockSpec((tile, width), lambda i, s: (i, 0))],
        [((rows, hidden), BF16, act)] * 3 + [((rows, width), BF16, pl.BlockSpec((rows, width), lambda i, s: (0, 0)))],
        [pltpu.VMEM((rows, width), F32)],
        chain,
        scalars,
        h2, wg, wu, wd,
    )


def finish_forward(chain, scalars, m, part, got, middle, cot, gain, step, output, prior):
    rows, width = part.shape
    steps = rows // step

    def body(sc, p_ref, q_ref, mid_ref, c_ref, g_ref, *refs):
        out_ref, d_ref, gain_ref = refs[-3:]

        @pl.when(pl.program_id(0) == 0)
        def _():
            begin(refs[:-3], gain_ref)

        ffn = p_ref[...].astype(F32) + q_ref[...].astype(F32)
        r3 = inv_rms(ffn)
        c = c_ref[...].astype(F32)
        n = ffn * r3
        out_ref[...] = (mid_ref[...] + n * one(g_ref, FFN_POST)).astype(BF16)
        d_ref[...] = pull_v(ffn, r3, one(g_ref, FFN_POST), c).astype(BF16)
        gain_ref[...] += jnp.sum(c * n, axis=0, keepdims=True)

    wide = pl.BlockSpec((step, width), lambda i, s: (i, 0))
    mine = pl.BlockSpec((step, width), lambda i, s: (m * steps + i, 0))
    return call(
        body,
        (steps,),
        [wide, wide, mine, mine, whole(gain)] + [whole(p) for p in prior],
        [
            (cot.shape, BF16, mine),
            ((rows, width), BF16, wide),
            ((1, width), F32, pl.BlockSpec((1, width), lambda i, s: (0, 0))),
        ],
        [],
        chain,
        scalars,
        part, got, middle, cot, gain, *prior,
        into={} if output is None else {0: output},
    )


def ffn_backward(chain, scalars, d_ffn, act, dact, wg, wu, wd, tile, chunk):
    width, hidden = wg.shape
    rows = d_ffn.shape[0]
    steps = hidden // tile

    def body(sc, d_ref, act_ref, dact_ref, wg_ref, wu_ref, wd_ref, dg_ref, du_ref, dh_ref, acc):
        @pl.when(pl.program_id(0) == 0)
        def _():
            acc[...] = jnp.zeros_like(acc)

        w = jnp.concatenate([wg_ref[...], wu_ref[...]], 1)
        for r in range(rows // chunk):
            at = pl.ds(r * chunk, chunk)
            dh = nt(d_ref[at, :], wd_ref[...])
            du = (dh * act_ref[at, :].astype(F32)).astype(BF16)
            dg = (dh * dact_ref[at, :].astype(F32)).astype(BF16)
            dg_ref[at, :] = dg
            du_ref[at, :] = du
            acc[at, :] += nt(jnp.concatenate([dg, du], 1), w)

        @pl.when(pl.program_id(0) == steps - 1)
        def _():
            dh_ref[...] = acc[...].astype(BF16)

    col = pl.BlockSpec((width, tile), lambda i, s: (0, i))
    acts = pl.BlockSpec((rows, tile), lambda i, s: (0, i))
    wide = pl.BlockSpec((rows, width), lambda i, s: (0, 0))
    return call(
        body,
        (steps,),
        [wide, acts, acts, col, col, pl.BlockSpec((tile, width), lambda i, s: (i, 0))],
        [((rows, hidden), BF16, acts), ((rows, hidden), BF16, acts), ((rows, width), BF16, wide)],
        [pltpu.VMEM((rows, width), F32)],
        chain,
        scalars,
        d_ffn, act, dact, wg, wu, wd,
    )


def attention_backward(chain, scalars, m, tensor_at, part, got, middle, cot, branch, gains, own, part_o, sibling_o, q, raw, head_gains,
                       cosine, sine, near, kv, prior):
    rows, width = part.shape
    per = own.shape[0] // HD
    heads = 2 * per

    def body(sc, p_ref, o_ref, mid_ref, c_ref, br_ref, g_ref, own_ref, part_ref, sib_ref, q_ref, raw_ref, gq_ref,
             cos_ref, sin_ref, nk_ref, k_ref, nv_ref, v_ref, *refs):
        (dm_ref, db_ref, dq_ref, dn_ref, dk_ref, dv_ref, sum_f_ref, sum_a_ref, sum_q_ref,
         near_bias, own_bias, near_kt, own_kt, acc) = refs[len(prior):]
        h = pl.program_id(0)

        @pl.when(h == 0)
        def _():
            set_bias(sc, m, near_bias, own_bias, True)
            near_kt[...] = nk_ref[...].T
            own_kt[...] = k_ref[...].T
            acc[...] = jnp.zeros_like(acc)
            begin(refs[:len(prior)], sum_f_ref, sum_a_ref, sum_q_ref)
            for r in range(rows // 128):
                at = pl.ds(r * 128, 128)
                e = p_ref[at, :].astype(F32) + o_ref[at, :].astype(F32)
                mid = mid_ref[at, :]
                r2 = inv_rms(mid)
                d_mid = c_ref[at, :].astype(F32) + pull_v(mid, r2, one(g_ref, FFN_IN), e)
                dm_ref[at, :] = d_mid
                sum_f_ref[...] += jnp.sum(e * mid * r2, axis=0, keepdims=True)
                branch = br_ref[at, :].astype(F32)
                r1 = inv_rms(branch)
                sum_a_ref[...] += jnp.sum(d_mid * branch * r1, axis=0, keepdims=True)
                db_ref[at, :] = pull_v(branch, r1, one(g_ref, ATTN_POST), d_mid).astype(BF16)

        other = jnp.where(h % per == sc[1], part_ref[...], sib_ref[...])
        wo = jnp.where(h // per == sc[tensor_at], own_ref[...], other)
        d_mix = nt(db_ref[...], wo).astype(BF16)
        qv = q_ref[...]
        near = jnp.exp(nt(nk_ref[...], qv) + near_bias[...])
        own = jnp.exp(nt(k_ref[...], qv) + own_bias[...])
        inv = 1.0 / (jnp.sum(near, axis=0, keepdims=True) + jnp.sum(own, axis=0, keepdims=True))
        near = near * inv
        own = own * inv
        acc[2] += nn(near.astype(BF16), d_mix)
        acc[3] += nn(own.astype(BF16), d_mix)
        dp_near = nt(nv_ref[...], d_mix)
        dp_own = nt(v_ref[...], d_mix)
        dots = jnp.sum(near * dp_near, axis=0, keepdims=True) + jnp.sum(own * dp_own, axis=0, keepdims=True)
        ds_near = (near * (dp_near - dots)).astype(BF16)
        ds_own = (own * (dp_own - dots)).astype(BF16)
        acc[0] += nn(ds_near, qv)
        acc[1] += nn(ds_own, qv)
        d_q = (nn(near_kt[...], ds_near) + nn(own_kt[...], ds_own)).T
        e_q = rotate_back(d_q * SCALE, cos_ref[...], sin_ref[...])
        raw_v = raw_ref[...].astype(F32)
        rq = inv_rms(raw_v)
        sum_q_ref[...] += jnp.sum(e_q * raw_v * rq, axis=0, keepdims=True)
        dq_ref[...] = pull_v(raw_v, rq, one(gq_ref, QUERY), e_q).astype(BF16)

        @pl.when(h == heads - 1)
        def _():
            dn_ref[:, :HD] = acc[0].astype(BF16)
            dk_ref[...] = acc[1]
            dn_ref[:, HD:] = acc[2].astype(BF16)
            dv_ref[...] = acc[3]

    wide = pl.BlockSpec((rows, width), lambda h, s: (0, 0))
    mine = pl.BlockSpec((rows, width), lambda h, s: (m, 0))
    key_at = pl.BlockSpec((rows, HD), lambda h, s: (m, 0))
    value_at = pl.BlockSpec((rows, HD), lambda h, s: (m, 1))
    heads_at = pl.BlockSpec((rows, HD), lambda h, s: (m, h))
    small = pl.BlockSpec((rows, HD), lambda h, s: (0, 0))
    sums = pl.BlockSpec((1, width), lambda h, s: (0, 0))
    weight = pl.BlockSpec((HD, width), lambda h, s: (h % per, 0))
    return call(
        body,
        (heads,),
        [wide, wide, mine, mine, mine, whole(gains), weight, whole(part_o), whole(sibling_o), heads_at, heads_at, whole(head_gains), whole(cosine), whole(sine),
         key_at, key_at, value_at, value_at] + [whole(p) for p in prior],
        [
            ((rows, width), F32, wide),
            ((rows, width), BF16, wide),
            ((rows, heads * HD), BF16, pl.BlockSpec((rows, HD), lambda h, s: (0, h))),
            ((rows, 2 * HD), BF16, pl.BlockSpec((rows, 2 * HD), lambda h, s: (0, 0))),
            ((rows, HD), F32, small),
            ((rows, HD), F32, small),
            ((1, width), F32, sums),
            ((1, width), F32, sums),
            ((1, HD), F32, pl.BlockSpec((1, HD), lambda h, s: (0, 0))),
        ],
        [pltpu.VMEM((rows, rows), F32)] * 2 + [pltpu.VMEM((HD, rows), BF16)] * 2 + [pltpu.VMEM((4, rows, HD), F32)],
        chain,
        scalars,
        part, got, middle, cot, branch, gains, own, part_o, sibling_o, q, raw, head_gains, cosine, sine,
        near, kv, near, kv, *prior,
    )


def input_gradient(chain, scalars, m, tensor_at, x, d_mid, dq, dk, dv, got, raw, head_gains, cosine, sine, wq, wk, wv, gains, step, grad, prior):
    rows, width = d_mid.shape
    steps = rows // step

    def body(sc, x_ref, dm_ref, dq_ref, dk_ref, dv_ref, gk_ref, gv_ref, raw_ref, g_ref, cos_ref, sin_ref,
             own_ref, part_ref, sib_ref, wk_ref, wv_ref, gain_ref, *refs):
        out_ref, kv_ref, sum_ref, sum_k_ref = refs[-4:]

        @pl.when(pl.program_id(0) == 0)
        def _():
            begin(refs[:-4], sum_ref, sum_k_ref)

        e = rotate_back(dk_ref[...] + gk_ref[...].astype(F32), cos_ref[...], sin_ref[...])
        raw_v = raw_ref[...]
        rk = inv_rms(raw_v)
        sum_k_ref[...] += jnp.sum(e * raw_v * rk, axis=0, keepdims=True)
        dkr = pull_v(raw_v, rk, one(g_ref, KEY), e).astype(BF16)
        dvr = (dv_ref[...] + gv_ref[...].astype(F32)).astype(BF16)
        kv_ref[:, :HD] = dkr
        kv_ref[:, HD:] = dvr
        other = joined(sc, part_ref[...], sib_ref[...])
        first, second = in_order(sc, tensor_at, own_ref[...], other)
        half = first.shape[1]
        d_h = nt(dq_ref[:, :half], first) + nt(dq_ref[:, half:], second) + nt(dkr, wk_ref[...]) + nt(dvr, wv_ref[...])
        v = x_ref[...].astype(F32)
        r0 = inv_rms(v)
        sum_ref[...] += jnp.sum(d_h * v * r0, axis=0, keepdims=True)
        out_ref[...] = dm_ref[...] + pull_v(v, r0, one(gain_ref, ATTN_IN), d_h)

    wide = pl.BlockSpec((step, width), lambda i, s: (i, 0))
    mine = pl.BlockSpec((step, width), lambda i, s: (m * steps + i, 0))
    head = pl.BlockSpec((step, HD), lambda i, s: (i, 0))
    table = pl.BlockSpec((step, HD // 2), lambda i, s: (i, 0))
    return call(
        body,
        (steps,),
        [mine, wide, pl.BlockSpec((step, dq.shape[1]), lambda i, s: (i, 0)), head, head, head,
         pl.BlockSpec((step, HD), lambda i, s: (i, 1)),
         pl.BlockSpec((step, HD), lambda i, s: (m * steps + i, 0)), whole(head_gains), table, table,
         *[whole(w) for w in wq], whole(wk), whole(wv), whole(gains), *[whole(p) for p in prior]],
        [
            (x.shape, F32, mine),
            ((rows, 2 * HD), BF16, pl.BlockSpec((step, 2 * HD), lambda i, s: (i, 0))),
            ((1, width), F32, pl.BlockSpec((1, width), lambda i, s: (0, 0))),
            ((1, HD), F32, pl.BlockSpec((1, HD), lambda i, s: (0, 0))),
        ],
        [],
        chain,
        scalars,
        x, d_mid, dq, dk, dv, got, got, raw, head_gains, cosine, sine, *wq, wk, wv, gains, *prior,
        into={} if grad is None else {0: grad},
    )


def weight_gradient(chain, scalars, lefts, rights, n, tile, tiles, chunk, right_at, out_at, out_tiles, into=None, extra=None):
    width = lefts[0][0].shape[1]
    rows = WINDOW
    rps = width // n
    count = len(lefts)

    def body(sc, *refs):
        l_refs, r_refs = refs[:count], refs[count:2 * count]
        send_ref, keep_ref, left_t = refs[-3:]

        @pl.when(pl.program_id(0) == 0)
        def _():
            for k in range(count):
                left_t[:, k * rows:(k + 1) * rows] = l_refs[k][...].T

        even = sc[1] == 0
        if extra is not None:
            filled = jnp.zeros((128 - extra.shape[0], width), F32)
            more_t = jnp.concatenate([refs[2 * count][...], filled], 0).T
        for c in range(width // chunk):
            v = nn(left_t[c * chunk:(c + 1) * chunk, :rows], r_refs[0][...])
            for k in range(1, count):
                v += nn(left_t[c * chunk:(c + 1) * chunk, k * rows:(k + 1) * rows], r_refs[k][...])
            if extra is not None:
                v = jnp.concatenate([v, more_t[c * chunk:(c + 1) * chunk]], 1)
            for j in range(chunk // (2 * rps)):
                a = v[2 * j * rps:(2 * j + 1) * rps]
                b = v[(2 * j + 1) * rps:(2 * j + 2) * rps]
                at = c * (chunk // (2 * rps)) + j
                send_ref[at] = jnp.where(even, b, a).astype(BF16)
                keep_ref[at] = jnp.where(even, a, b).astype(BF16)

    more = 0 if extra is None else 128
    out = pl.BlockSpec((n // 2, rps, tile + more), lambda i, s: (0, 0, out_at + i))
    shape = (n // 2, rps, out_tiles * tile + more)

    def left_spec(at):
        return pl.BlockSpec((rows, width), lambda i, s: (at, 0))

    def right_spec(at):
        return pl.BlockSpec((rows, tile), lambda i, s: (at, right_at(s) + i))

    return call(
        body,
        (tiles,),
        [left_spec(at) for _, at in lefts] + [right_spec(at) for _, at in rights]
        + ([] if extra is None else [whole(extra)]),
        [(shape, BF16, out), (shape, BF16, out)],
        [pltpu.VMEM((width, count * rows), BF16)],
        chain,
        scalars,
        *[l for l, _ in lefts], *[r for r, _ in rights], *([] if extra is None else [extra]),
        into=None if into is None else {0: into[0], 1: into[1]},
    )


def plain_gradient(lefts, rights, n, tile, tiles, start, extra=None):
    width = lefts[0][0].shape[1]
    total = 0.0
    for (left, la), (right, ra) in zip(lefts, rights):
        left = left[la * WINDOW:(la + 1) * WINDOW]
        right = lax.dynamic_slice_in_dim(right[ra * WINDOW:(ra + 1) * WINDOW], start * tile, tile * tiles, 1)
        total = total + lax.dot_general(left, right, (((0,), (0,)), ((), ())), preferred_element_type=F32)
    if extra is not None:
        total = jnp.concatenate([total, jnp.pad(extra.T, ((0, 0), (0, 120)))], 1)
    both = total.astype(BF16).reshape(n // 2, 2, width // n, -1)
    core = my_bit(0)
    return (
        lax.dynamic_index_in_dim(both, 1 - core, 1, keepdims=False),
        lax.dynamic_index_in_dim(both, core, 1, keepdims=False),
    )


class Halving:
    def __init__(self, chain, at, send, keep, order):
        self.chain = chain
        self.at = at
        self.sum = None
        self.bits = list(range(1, lax.axis_size("dp").bit_length() - 1))[::-1]
        self.order = list(order)
        shape = (2,) * len(self.bits) + keep.shape[1:]
        self.parts = [(keep.reshape(shape), self.bits), (chain.moved(swap_dp(send, 0)).reshape(shape), self.bits)]

    def job(self):
        bit = self.order.pop(0) if self.order else None
        self.bits = [b for b in self.bits if b != bit]
        rps, columns = self.parts[0][0].shape[-2:]
        bits, at = self.bits if bit is not None else [], self.at

        def block_at(p_bits, tile):
            def index(j, s):
                def value(b):
                    mine = (s[at] >> b) & 1
                    return 1 - mine if b == bit else mine

                return tuple(0 if b in bits else value(b) for b in p_bits) + (0, j)

            return pl.BlockSpec(tuple(2 if b in bits else None for b in p_bits) + (rps, tile), index)

        def done(out):
            if bit is None:
                self.sum = out
            else:
                self.parts.append((self.chain.moved(swap_dp(out, bit)), bits))

        dtype = F32 if bit is None else BF16
        shape = (2,) * len(bits) + (rps, columns)
        return self.parts[:], block_at, shape, dtype, done


def add_parts(chain, scalars, *halvings, handed=None):
    jobs = [h.job() for h in halvings]
    steps = 1 if all(j[2][-1] % 384 == 0 for j in jobs) else 1
    ins, outs, args = [], [], []
    for parts, block_at, shape, dtype, _ in jobs:
        tile = shape[-1] // steps
        lead = shape[:-2]
        args += [p for p, _ in parts]
        ins += [block_at(bits, tile) for _, bits in parts]
        spec = pl.BlockSpec(shape[:-1] + (tile,), lambda j, s, z=(0,) * (len(lead) + 1): z + (j,))
        outs.append((shape, dtype, spec))

    more = {}
    if handed is not None:
        outs.insert(0, (handed.shape, handed.dtype, pl.BlockSpec(memory_space=pl.ANY)))
        more = dict(into={0: handed}, ahead=chain.received)

    def body(sc, *refs):
        left = refs[:len(args)]
        for (parts, _, _, dtype, _), out in zip(jobs, refs[len(refs) - len(jobs):]):
            total = left[0][...].astype(F32)
            for r in left[1:len(parts)]:
                total += r[...].astype(F32)
            out[...] = total.astype(dtype)
            left = left[len(parts):]

    results = call(body, (steps,), ins, outs, [], chain, scalars, *args, **more)
    if handed is not None:
        handed, *results = results
    for (_, _, _, _, done), out in zip(jobs, results):
        done(out)
    return handed


def shards(
    tokens,
    image_starts,
    g_attn_in,
    w_query,
    w_key,
    w_value,
    g_query,
    g_key,
    w_out,
    g_attn_post,
    g_ffn_in,
    w_gate,
    w_up,
    w_down,
    g_ffn_post,
    cotangent,
):
    mb, rows, width = tokens.shape
    own = w_query.shape[1]
    y = lax.axis_index("tensor")
    dp = lax.axis_index("dp")
    n = lax.axis_size("dp")
    offset = dp % (SEQ_LEN // rows) * rows
    cosine, sine = angle_tables(offset + jnp.arange(rows, dtype=jnp.int32))
    core = my_bit(0)
    scalars = jnp.concatenate([jnp.stack([offset, core]), image_starts[:, 0], jnp.stack([y, dp])]).astype(jnp.int32)
    low_first = list(range(1, n.bit_length() - 1))
    low_last = low_first[1:] + low_first[:1]

    x = tokens.reshape(mb * rows, width)
    cot = cotangent.reshape(mb * rows, width)
    chain = Chain()

    gains = jnp.stack([g_attn_in, g_attn_post, g_ffn_in, g_ffn_post])
    head_gains = jnp.stack([g_query, g_key])
    tensor_at = 2 + mb
    part_q = chain.moved(swap_y(pick(w_query.reshape(2, width // 2, own), core)))
    h1, key_raw, kv = pre_attention(
        chain, scalars, x, gains, w_key, w_value, head_gains, cosine, sine, rows
    )
    near = chain.moved(shift_dp(kv, 1))
    sibling_q = chain.moved(swap_dp(after(part_q, kv), 0))
    part_o = chain.moved(swap_y(pick(after(w_out, part_q).reshape(2, own // 2, width), core)))
    pair = None
    for other in (None, (part_q, sibling_q)):
        pair = queries(
            chain, scalars, tensor_at, h1, w_query, other, head_gains, cosine, sine, rows, pair
        )
    query_raw, query = pair
    mixed = attention(chain, scalars, query, near, kv, rows)
    sibling_o = chain.moved(swap_dp(after(part_o, mixed), 0))
    other_o = (part_o, sibling_o)
    branch, middle, h2 = post_attention(
        chain, scalars, tensor_at, x, mixed, w_out, *other_o, gains, rows // 2
    )

    forward = []
    for m in range(mb):
        act, dact, hidden, part = ffn_forward(chain, scalars, m, h2, w_gate, w_up, w_down, rows, 1152, 256)
        forward.append((act, dact, hidden, part, chain.moved(swap_y(part))))

    split = width // n % 8 == 0
    hidden_width = w_gate.shape[1]

    def gradient(lefts, rights, tile, tiles, first=0, own_tile=False, out_at=0, out_tiles=None, into=None, extra=None):
        if split:
            right_at = (lambda s: s[tensor_at]) if own_tile else (lambda s: first)
            return weight_gradient(
                chain, scalars, lefts, rights, n, tile, tiles, 576, right_at, out_at, out_tiles or tiles, into, extra
            )
        made = plain_gradient(lefts, rights, n, tile, tiles, y if own_tile else first, extra)
        if into is None:
            return made
        return tuple(jnp.concatenate(p, -1) for p in zip(into, made))

    def batches(a):
        return [(a, m) for m in range(mb)]

    def each(arrays):
        return [(a, 0) for a in arrays]

    def halving(pair, order):
        return Halving(chain, 3 + mb, *pair, order)

    def serve(*halvings, handed=None):
        for h in halvings[:-1]:
            add_parts(chain, scalars, h)
        return add_parts(chain, scalars, halvings[-1], handed=handed)

    output = None
    d_ffns, grads, parts = [], [], []
    post_sum = ()
    hiddens = each([f[2] for f in forward])
    for m in range(mb):
        act, dact, hidden, part, got = forward[m]
        output, d_ffn, *post_sum = finish_forward(
            chain, scalars, m, part, got, middle, cot, gains, rows // 2, output, post_sum
        )
        d_ffns.append(d_ffn)
        if m == mb - 1:
            down = halving(gradient(each(d_ffns), hiddens, 1152, 3), low_last)
        d_gate, d_up, dh = ffn_backward(chain, scalars, d_ffn, act, dact, w_gate, w_up, w_down, 1152, 256)
        grads.append((d_gate, d_up))
        parts.append((dh, chain.moved(swap_y(dh))))

    serve(down)
    gate = halving(gradient(batches(h2), each([g[0] for g in grads]), 1152, 3), low_first)
    up = halving(gradient(batches(h2), each([g[1] for g in grads]), 1152, 3), low_first)
    serve(gate)
    chain.before_next(parts[1][1])

    back = []
    shifted = []
    for m in range(mb):
        back.append(
            attention_backward(
                chain, scalars, m, tensor_at, *parts[m], middle, cot, branch, gains, w_out, *other_o, query,
                query_raw, head_gains, cosine, sine, near, kv, back[-1][6:] if back else (),
            )
        )
        shifted.append(chain.moved(shift_dp(back[m][3], -1)))
        if m == 0:
            serve(down)
    serve(up)
    chain.before_next(shifted[0])
    own_at = dict(own_tile=True, out_tiles=2)
    pair = gradient(each([b[1] for b in back]), batches(mixed), own, 1, **own_at)
    pair = gradient(batches(h1), each([b[2] for b in back]), own, 1, out_at=1, into=pair, **own_at)
    attn = halving(pair, low_first)
    serve(gate)

    grad_input = None
    kvs = []
    in_sums = ()
    for m in range(mb):
        d_mid, d_branch, dq, _, dk, dv = back[m][:6]
        grad_input, dkv, *in_sums = input_gradient(
            chain, scalars, m, tensor_at, x, d_mid, dq, dk, dv, shifted[m], key_raw, head_gains, cosine, sine,
            (w_query, part_q, sibling_q), w_key, w_value, gains, rows // 2, grad_input, in_sums,
        )
        kvs.append(dkv)
        if m == 0:
            serve(down, attn, gate, up)

    rps = width // n
    hps = HD // n

    def spread(sums):
        return jnp.pad(sums.reshape(n, hps), ((0, 0), (0, rps - hps))).reshape(1, width)

    extra = jnp.concatenate(
        [
            in_sums[0],
            post_sum[0],
            back[-1][6],
            back[-1][7],
            spread(back[-1][8]),
            spread(in_sums[1]),
            jnp.zeros((2, width), F32),
        ]
    )
    last = halving(gradient(batches(h1), each(kvs), 2 * HD, 1, extra=extra), low_first)
    serve(attn, last, up, down, last, attn, gate, last)
    every = (attn, down, gate, up, last)
    while last.order:
        serve(*[h for h in every if h.order])
    output = serve(*[h for h in every if h.sum is None], handed=output)
    last, grad_attn = last.sum, attn.sum
    gain_grads = last[:, 2 * HD:]
    return (
        output.reshape(tokens.shape),
        grad_input.reshape(tokens.shape),
        gain_grads[:, 0],
        grad_attn[:, own:],
        last[:, :HD],
        last[:, HD:2 * HD],
        gain_grads[:hps, 4],
        gain_grads[:hps, 5],
        grad_attn[:, :own].T,
        gain_grads[:, 3],
        gain_grads[:, 2],
        gate.sum,
        up.sum,
        down.sum.T,
        gain_grads[:, 1],
    )


def solution(mesh):
    rows = P(None, "dp", None)
    in_specs = (
        rows,
        P(None, "dp"),
        P(),
        P(None, "tensor"),
        P(),
        P(),
        P(),
        P(),
        P("tensor", None),
        P(),
        P(),
        P(None, "tensor"),
        P(None, "tensor"),
        P("tensor", None),
        P(),
        rows,
    )
    out_specs = (
        rows,
        rows,
        P("dp"),
        P("dp", "tensor"),
        P("dp", None),
        P("dp", None),
        P("dp"),
        P("dp"),
        P("tensor", "dp"),
        P("dp"),
        P("dp"),
        P("dp", "tensor"),
        P("dp", "tensor"),
        P("tensor", "dp"),
        P("dp"),
    )
    return jax.shard_map(shards, mesh=mesh, in_specs=in_specs, out_specs=out_specs, check_vma=False)
```

```python
import jax
import jax.numpy as jnp
from jax import lax
from jax.experimental import pallas as pl
from jax.experimental.pallas import tpu as pltpu
from jax.sharding import PartitionSpec as P
import numpy as np

HD = 256
WINDOW = 512
IMG = 256
SEQ_LEN = 4096
EPSILON = 1e-06
NEGATIVE = -1e30
SCALE = HD ** -0.5
GELU_C = 0.7978845608028654
GELU_A = 0.044715
F32 = jnp.float32
BF16 = jnp.bfloat16
VMEM_BYTES = 60 * 2**20
ATTN_IN, ATTN_POST, FFN_IN, FFN_POST = range(4)
QUERY, KEY = range(2)


def nn(a, b):
    return jnp.dot(a, b, preferred_element_type=F32)


def nt(a, b):
    return lax.dot_general(a, b, (((1,), (1,)), ((), ())), preferred_element_type=F32)


def inv_rms(v):
    return lax.rsqrt(jnp.mean(v * v, axis=-1, keepdims=True) + EPSILON)


def pull_v(v, r, g, e):
    eg = e * g
    return r * eg - v * (r * r * r * jnp.mean(v * eg, axis=-1, keepdims=True))


def rotate(v, cosine, sine):
    half = v.shape[-1] // 2
    a, b = v[:, :half], v[:, half:]
    return jnp.concatenate([a * cosine - b * sine, b * cosine + a * sine], axis=-1)


def rotate_back(v, cosine, sine):
    half = v.shape[-1] // 2
    a, b = v[:, :half], v[:, half:]
    return jnp.concatenate([a * cosine + b * sine, b * cosine - a * sine], axis=-1)


def angle_tables(places):
    half = HD // 2
    frequency = (10000.0 ** (-2.0 * np.arange(half) / HD)).astype(np.float32)
    angles = places.astype(F32)[:, None] * frequency[None, :]
    return jnp.cos(angles), jnp.sin(angles)


def swap_y(v):
    return lax.ppermute(v, "tensor", [(0, 1), (1, 0)])


def swap_dp(v, bit):
    n = lax.axis_size("dp")
    return lax.ppermute(v, "dp", [(i, i ^ (1 << bit)) for i in range(n)])


def shift_dp(v, steps):
    n = lax.axis_size("dp")
    first, last = max(0, -steps), min(n, n - steps)
    return lax.ppermute(v, "dp", [(i, i + steps) for i in range(first, last)])


def my_bit(bit):
    return (lax.axis_index("dp") >> bit) & 1


def after(value, *earlier):
    return lax.optimization_barrier((value,) + earlier)[0]


def pick(a, i):
    return lax.dynamic_index_in_dim(a, i, 0, keepdims=False)


class Chain:
    def __init__(self):
        self.last = ()
        self.first = []
        self.received = []

    def before_next(self, *arrays):
        self.first.extend(arrays)

    def moved(self, array):
        self.received.append(array)
        return array

    def take(self):
        taken, self.first = list(self.last) + self.first, []
        return taken


def call(body, grid, ins, outs, scratch, chain, scalars, *args, into=None, ahead=()):
    count = len(ins)
    ahead = list(ahead)
    skip = len(ahead)
    into = into or {}
    given = list(into.values())
    extra = given + [a for a in chain.take() if not any(a is g for g in given)]
    aliases = {1 + skip + count + k: out for k, out in enumerate(into)}

    anywhere = pl.BlockSpec(memory_space=pl.ANY)

    def inner(sc, *refs):
        body(sc, *refs[skip:skip + count], *refs[skip + count + len(extra):])

    results = pl.pallas_call(
        inner,
        grid_spec=pltpu.PrefetchScalarGridSpec(
            num_scalar_prefetch=1,
            grid=grid,
            in_specs=[anywhere] * skip + list(ins) + [anywhere] * len(extra),
            out_specs=[o[2] for o in outs],
            scratch_shapes=scratch,
        ),
        out_shape=[jax.ShapeDtypeStruct(s, d) for s, d, _ in outs],
        input_output_aliases=aliases,
        compiler_params=pltpu.CompilerParams(
            vmem_limit_bytes=VMEM_BYTES,
            dimension_semantics=("arbitrary",) * len(grid),
        ),
        cost_estimate=pl.CostEstimate(flops=10**14, bytes_accessed=1000, transcendentals=0),
    )(scalars, *ahead, *args, *extra)
    chain.last = (min(results, key=lambda r: r.size),)
    return results


def begin(prior, *sums):
    for k, s in enumerate(sums):
        s[...] = prior[k][...] if prior else jnp.zeros_like(s)


def one(ref, k):
    return ref[k:k + 1, :]


def whole(a):
    nd = len(a.shape)
    return pl.BlockSpec(a.shape, lambda *i: (0,) * nd)


def in_order(sc, at, own, other):
    first = sc[at] == 0
    return jnp.where(first, own, other), jnp.where(first, other, own)


def joined(sc, part, sibling):
    first = sc[1] == 0
    return jnp.concatenate([jnp.where(first, part, sibling), jnp.where(first, sibling, part)], 0)


def pre_attention(chain, scalars, x, gain, wk, wv, g_key, cosine, sine, step):
    total, width = x.shape
    rows = cosine.shape[0]

    def body(sc, x_ref, g_ref, wk_ref, wv_ref, gk_ref, cos_ref, sin_ref, h_ref, raw_ref, kv_ref):
        v = x_ref[...].astype(F32)
        h = (v * inv_rms(v) * one(g_ref, ATTN_IN)).astype(BF16)
        h_ref[...] = h
        raw = nn(h, wk_ref[...])
        raw_ref[...] = raw
        key = rotate(raw * inv_rms(raw) * one(gk_ref, KEY), cos_ref[...], sin_ref[...])
        kv_ref[:, :HD] = key.astype(BF16)
        kv_ref[:, HD:] = nn(h, wv_ref[...]).astype(BF16)

    per = rows // step
    table = pl.BlockSpec((step, HD // 2), lambda i, s: (i % per, 0))
    wide = pl.BlockSpec((step, width), lambda i, s: (i, 0))
    head = pl.BlockSpec((step, HD), lambda i, s: (i, 0))
    return call(
        body,
        (total // step,),
        [wide, whole(gain), whole(wk), whole(wv), whole(g_key), table, table],
        [
            ((total, width), BF16, wide),
            ((total, HD), F32, head),
            ((total, 2 * HD), BF16, pl.BlockSpec((step, 2 * HD), lambda i, s: (i, 0))),
        ],
        [],
        chain,
        scalars,
        x, gain, wk, wv, g_key, cosine, sine,
    )


def set_bias(sc, m, near_ref, own_ref, transposed):
    rows = near_ref.shape[0]
    q_dim, k_dim = (1, 0) if transposed else (0, 1)
    q = lax.broadcasted_iota(jnp.int32, (rows, rows), q_dim)
    k = lax.broadcasted_iota(jnp.int32, (rows, rows), k_dim)
    start = sc[2 + m]
    after = (k > q) & (sc[0] > 0)
    near_ref[...] = jnp.where(after, 0.0, NEGATIVE)
    in_q = (q >= start) & (q < start + IMG)
    in_k = (k >= start) & (k < start + IMG)
    own_ref[...] = jnp.where((k <= q) | (in_q & in_k), 0.0, NEGATIVE)


def queries(chain, scalars, at, h1, own, other, gains, cosine, sine, step, into):
    total, width = h1.shape
    columns = own.shape[1]
    weights = [own] if other is None else list(other)

    def body(sc, h_ref, *refs):
        w_refs = refs[:len(weights)]
        g_ref, cos_ref, sin_ref, raw_ref, q_ref = refs[len(weights):]
        w = w_refs[0][...] if other is None else joined(sc, w_refs[0][...], w_refs[1][...])
        both = nn(h_ref[...], w)
        raw_ref[...] = both.astype(BF16)
        for k in range(columns // HD):
            raw = both[:, k * HD:(k + 1) * HD]
            q = rotate(raw * inv_rms(raw) * one(g_ref, QUERY), cos_ref[...], sin_ref[...]) * SCALE
            q_ref[:, k * HD:(k + 1) * HD] = q.astype(BF16)

    per = cosine.shape[0] // step
    table = pl.BlockSpec((step, HD // 2), lambda i, s: (i % per, 0))
    out = pl.BlockSpec((step, columns), lambda i, s: (i, s[at] if other is None else 1 - s[at]))
    shape = (total, 2 * columns)
    return call(
        body,
        (total // step,),
        [pl.BlockSpec((step, width), lambda i, s: (i, 0))] + [whole(w) for w in weights]
        + [whole(gains), table, table],
        [(shape, BF16, out)] * 2,
        [],
        chain,
        scalars,
        h1, *weights, gains, cosine, sine,
        into={} if into is None else {0: into[0], 1: into[1]},
    )


def attention(chain, scalars, query, near, kv, rows):
    total = query.shape[0]
    heads = query.shape[1] // HD

    def body(sc, q_ref, nk_ref, k_ref, nv_ref, v_ref, mix_ref, near_bias, own_bias):
        @pl.when(pl.program_id(1) == 0)
        def _():
            set_bias(sc, pl.program_id(0), near_bias, own_bias, False)

        q = q_ref[...]
        near = jnp.exp(nt(q, nk_ref[...]) + near_bias[...])
        own = jnp.exp(nt(q, k_ref[...]) + own_bias[...])
        sums = jnp.sum(near, axis=-1, keepdims=True) + jnp.sum(own, axis=-1, keepdims=True)
        mix = nn(near.astype(BF16), nv_ref[...]) + nn(own.astype(BF16), v_ref[...])
        mix_ref[...] = (mix / sums).astype(BF16)

    key_at = pl.BlockSpec((rows, HD), lambda m, h, s: (m, 0))
    value_at = pl.BlockSpec((rows, HD), lambda m, h, s: (m, 1))
    out = pl.BlockSpec((rows, HD), lambda m, h, s: (m, h))
    return call(
        body,
        (total // rows, heads),
        [out, key_at, key_at, value_at, value_at],
        [(query.shape, BF16, out)],
        [pltpu.VMEM((rows, rows), F32)] * 2,
        chain,
        scalars,
        query, near, kv, near, kv,
    )[0]


def post_attention(chain, scalars, tensor_at, x, mixed, own, part, sibling, gains, step):
    total, width = x.shape

    def body(sc, x_ref, m_ref, own_ref, part_ref, sib_ref, g_ref, br_ref, mid_ref, h_ref):
        other = joined(sc, part_ref[...], sib_ref[...])
        first, second = in_order(sc, tensor_at, own_ref[...], other)
        branch = nn(m_ref[:, :half], first) + nn(m_ref[:, half:], second)
        br_ref[...] = branch.astype(BF16)
        middle = x_ref[...].astype(F32) + branch * inv_rms(branch) * one(g_ref, ATTN_POST)
        mid_ref[...] = middle.astype(BF16)
        h_ref[...] = (middle * inv_rms(middle) * one(g_ref, FFN_IN)).astype(BF16)

    half = own.shape[0]
    wide = pl.BlockSpec((step, width), lambda i, s: (i, 0))
    shape = (total, width)
    return call(
        body,
        (total // step,),
        [wide, pl.BlockSpec((step, mixed.shape[1]), lambda i, s: (i, 0)), whole(own), whole(part), whole(sibling), whole(gains)],
        [(shape, BF16, wide)] * 3,
        [],
        chain,
        scalars,
        x, mixed, own, part, sibling, gains,
    )


def ffn_forward(chain, scalars, m, h2, wg, wu, wd, rows, tile, chunk):
    width, hidden = wg.shape
    steps = hidden // tile

    def body(sc, h_ref, wg_ref, wu_ref, wd_ref, act_ref, dact_ref, hid_ref, out_ref, acc):
        @pl.when(pl.program_id(0) == 0)
        def _():
            acc[...] = jnp.zeros_like(acc)

        w = jnp.concatenate([wg_ref[...], wu_ref[...]], 1)
        for r in range(rows // chunk):
            at = pl.ds(r * chunk, chunk)
            both = nn(h_ref[at, :], w)
            g, u = both[:, :tile], both[:, tile:]
            g2 = g * g
            t = jnp.tanh(g * (GELU_C + GELU_C * GELU_A * g2))
            half = 0.5 + 0.5 * t
            act = g * half
            dact = half + 0.5 * g * (1.0 - t * t) * (GELU_C + 3.0 * GELU_C * GELU_A * g2)
            act_ref[at, :] = act.astype(BF16)
            dact_ref[at, :] = (dact * u).astype(BF16)
            hid = (act * u).astype(BF16)
            hid_ref[at, :] = hid
            acc[at, :] += nn(hid, wd_ref[...])

        @pl.when(pl.program_id(0) == steps - 1)
        def _():
            out_ref[...] = acc[...].astype(BF16)

    col = pl.BlockSpec((width, tile), lambda i, s: (0, i))
    act = pl.BlockSpec((rows, tile), lambda i, s: (0, i))
    return call(
        body,
        (steps,),
        [pl.BlockSpec((rows, width), lambda i, s: (m, 0)), col, col, pl.BlockSpec((tile, width), lambda i, s: (i, 0))],
        [((rows, hidden), BF16, act)] * 3 + [((rows, width), BF16, pl.BlockSpec((rows, width), lambda i, s: (0, 0)))],
        [pltpu.VMEM((rows, width), F32)],
        chain,
        scalars,
        h2, wg, wu, wd,
    )


def finish_forward(chain, scalars, m, part, got, middle, cot, gain, step, output, prior):
    rows, width = part.shape
    steps = rows // step

    def body(sc, p_ref, q_ref, mid_ref, c_ref, g_ref, *refs):
        out_ref, d_ref, gain_ref = refs[-3:]

        @pl.when(pl.program_id(0) == 0)
        def _():
            begin(refs[:-3], gain_ref)

        ffn = p_ref[...].astype(F32) + q_ref[...].astype(F32)
        r3 = inv_rms(ffn)
        c = c_ref[...].astype(F32)
        n = ffn * r3
        out_ref[...] = (mid_ref[...].astype(F32) + n * one(g_ref, FFN_POST)).astype(BF16)
        d_ref[...] = pull_v(ffn, r3, one(g_ref, FFN_POST), c).astype(BF16)
        gain_ref[...] += jnp.sum(c * n, axis=0, keepdims=True)

    wide = pl.BlockSpec((step, width), lambda i, s: (i, 0))
    mine = pl.BlockSpec((step, width), lambda i, s: (m * steps + i, 0))
    return call(
        body,
        (steps,),
        [wide, wide, mine, mine, whole(gain)] + [whole(p) for p in prior],
        [
            (cot.shape, BF16, mine),
            ((rows, width), BF16, wide),
            ((1, width), F32, pl.BlockSpec((1, width), lambda i, s: (0, 0))),
        ],
        [],
        chain,
        scalars,
        part, got, middle, cot, gain, *prior,
        into={} if output is None else {0: output},
    )


def ffn_backward(chain, scalars, d_ffn, act, dact, wg, wu, wd, tile, chunk):
    width, hidden = wg.shape
    rows = d_ffn.shape[0]
    steps = hidden // tile

    def body(sc, d_ref, act_ref, dact_ref, wg_ref, wu_ref, wd_ref, dg_ref, du_ref, dh_ref, acc):
        @pl.when(pl.program_id(0) == 0)
        def _():
            acc[...] = jnp.zeros_like(acc)

        w = jnp.concatenate([wg_ref[...], wu_ref[...]], 1)
        for r in range(rows // chunk):
            at = pl.ds(r * chunk, chunk)
            dh = nt(d_ref[at, :], wd_ref[...])
            du = (dh * act_ref[at, :].astype(F32)).astype(BF16)
            dg = (dh * dact_ref[at, :].astype(F32)).astype(BF16)
            dg_ref[at, :] = dg
            du_ref[at, :] = du
            acc[at, :] += nt(jnp.concatenate([dg, du], 1), w)

        @pl.when(pl.program_id(0) == steps - 1)
        def _():
            dh_ref[...] = acc[...].astype(BF16)

    col = pl.BlockSpec((width, tile), lambda i, s: (0, i))
    acts = pl.BlockSpec((rows, tile), lambda i, s: (0, i))
    wide = pl.BlockSpec((rows, width), lambda i, s: (0, 0))
    return call(
        body,
        (steps,),
        [wide, acts, acts, col, col, pl.BlockSpec((tile, width), lambda i, s: (i, 0))],
        [((rows, hidden), BF16, acts), ((rows, hidden), BF16, acts), ((rows, width), BF16, wide)],
        [pltpu.VMEM((rows, width), F32)],
        chain,
        scalars,
        d_ffn, act, dact, wg, wu, wd,
    )


def attention_backward(chain, scalars, m, tensor_at, part, got, middle, cot, branch, gains, own, part_o, sibling_o, q, raw, head_gains,
                       cosine, sine, near, kv, prior):
    rows, width = part.shape
    per = own.shape[0] // HD
    heads = 2 * per

    def body(sc, p_ref, o_ref, mid_ref, c_ref, br_ref, g_ref, own_ref, part_ref, sib_ref, q_ref, raw_ref, gq_ref,
             cos_ref, sin_ref, nk_ref, k_ref, nv_ref, v_ref, *refs):
        (dm_ref, db_ref, dq_ref, dn_ref, dk_ref, dv_ref, sum_f_ref, sum_a_ref, sum_q_ref,
         near_bias, own_bias, near_kt, own_kt, acc) = refs[len(prior):]
        h = pl.program_id(0)

        @pl.when(h == 0)
        def _():
            set_bias(sc, m, near_bias, own_bias, True)
            near_kt[...] = nk_ref[...].T
            own_kt[...] = k_ref[...].T
            acc[...] = jnp.zeros_like(acc)
            begin(refs[:len(prior)], sum_f_ref, sum_a_ref, sum_q_ref)
            for r in range(rows // 128):
                at = pl.ds(r * 128, 128)
                e = p_ref[at, :].astype(F32) + o_ref[at, :].astype(F32)
                mid = mid_ref[at, :].astype(F32)
                r2 = inv_rms(mid)
                d_mid = c_ref[at, :].astype(F32) + pull_v(mid, r2, one(g_ref, FFN_IN), e)
                dm_ref[at, :] = d_mid.astype(BF16)
                sum_f_ref[...] += jnp.sum(e * mid * r2, axis=0, keepdims=True)
                branch = br_ref[at, :].astype(F32)
                r1 = inv_rms(branch)
                sum_a_ref[...] += jnp.sum(d_mid * branch * r1, axis=0, keepdims=True)
                db_ref[at, :] = pull_v(branch, r1, one(g_ref, ATTN_POST), d_mid).astype(BF16)

        other = jnp.where(h % per == sc[1], part_ref[...], sib_ref[...])
        wo = jnp.where(h // per == sc[tensor_at], own_ref[...], other)
        d_mix = nt(db_ref[...], wo).astype(BF16)
        qv = q_ref[...]
        near = jnp.exp(nt(nk_ref[...], qv) + near_bias[...])
        own = jnp.exp(nt(k_ref[...], qv) + own_bias[...])
        inv = 1.0 / (jnp.sum(near, axis=0, keepdims=True) + jnp.sum(own, axis=0, keepdims=True))
        near = near * inv
        own = own * inv
        acc[2] += nn(near.astype(BF16), d_mix)
        acc[3] += nn(own.astype(BF16), d_mix)
        dp_near = nt(nv_ref[...], d_mix)
        dp_own = nt(v_ref[...], d_mix)
        dots = jnp.sum(near * dp_near, axis=0, keepdims=True) + jnp.sum(own * dp_own, axis=0, keepdims=True)
        ds_near = (near * (dp_near - dots)).astype(BF16)
        ds_own = (own * (dp_own - dots)).astype(BF16)
        acc[0] += nn(ds_near, qv)
        acc[1] += nn(ds_own, qv)
        d_q = (nn(near_kt[...], ds_near) + nn(own_kt[...], ds_own)).T
        e_q = rotate_back(d_q * SCALE, cos_ref[...], sin_ref[...])
        raw_v = raw_ref[...].astype(F32)
        rq = inv_rms(raw_v)
        sum_q_ref[...] += jnp.sum(e_q * raw_v * rq, axis=0, keepdims=True)
        dq_ref[...] = pull_v(raw_v, rq, one(gq_ref, QUERY), e_q).astype(BF16)

        @pl.when(h == heads - 1)
        def _():
            dn_ref[:, :HD] = acc[0].astype(BF16)
            dk_ref[...] = acc[1]
            dn_ref[:, HD:] = acc[2].astype(BF16)
            dv_ref[...] = acc[3]

    wide = pl.BlockSpec((rows, width), lambda h, s: (0, 0))
    mine = pl.BlockSpec((rows, width), lambda h, s: (m, 0))
    key_at = pl.BlockSpec((rows, HD), lambda h, s: (m, 0))
    value_at = pl.BlockSpec((rows, HD), lambda h, s: (m, 1))
    heads_at = pl.BlockSpec((rows, HD), lambda h, s: (m, h))
    small = pl.BlockSpec((rows, HD), lambda h, s: (0, 0))
    sums = pl.BlockSpec((1, width), lambda h, s: (0, 0))
    weight = pl.BlockSpec((HD, width), lambda h, s: (h % per, 0))
    return call(
        body,
        (heads,),
        [wide, wide, mine, mine, mine, whole(gains), weight, whole(part_o), whole(sibling_o), heads_at, heads_at, whole(head_gains), whole(cosine), whole(sine),
         key_at, key_at, value_at, value_at] + [whole(p) for p in prior],
        [
            ((rows, width), BF16, wide),
            ((rows, width), BF16, wide),
            ((rows, heads * HD), BF16, pl.BlockSpec((rows, HD), lambda h, s: (0, h))),
            ((rows, 2 * HD), BF16, pl.BlockSpec((rows, 2 * HD), lambda h, s: (0, 0))),
            ((rows, HD), F32, small),
            ((rows, HD), F32, small),
            ((1, width), F32, sums),
            ((1, width), F32, sums),
            ((1, HD), F32, pl.BlockSpec((1, HD), lambda h, s: (0, 0))),
        ],
        [pltpu.VMEM((rows, rows), F32)] * 2 + [pltpu.VMEM((HD, rows), BF16)] * 2 + [pltpu.VMEM((4, rows, HD), F32)],
        chain,
        scalars,
        part, got, middle, cot, branch, gains, own, part_o, sibling_o, q, raw, head_gains, cosine, sine,
        near, kv, near, kv, *prior,
    )


def input_gradient(chain, scalars, m, tensor_at, x, d_mid, dq, dk, dv, got, raw, head_gains, cosine, sine, wq, wk, wv, gains, step, grad, prior):
    rows, width = d_mid.shape
    steps = rows // step

    def body(sc, x_ref, dm_ref, dq_ref, dk_ref, dv_ref, gk_ref, gv_ref, raw_ref, g_ref, cos_ref, sin_ref,
             own_ref, part_ref, sib_ref, wk_ref, wv_ref, gain_ref, *refs):
        out_ref, kv_ref, sum_ref, sum_k_ref = refs[-4:]

        @pl.when(pl.program_id(0) == 0)
        def _():
            begin(refs[:-4], sum_ref, sum_k_ref)

        e = rotate_back(dk_ref[...] + gk_ref[...].astype(F32), cos_ref[...], sin_ref[...])
        raw_v = raw_ref[...]
        rk = inv_rms(raw_v)
        sum_k_ref[...] += jnp.sum(e * raw_v * rk, axis=0, keepdims=True)
        dkr = pull_v(raw_v, rk, one(g_ref, KEY), e).astype(BF16)
        dvr = (dv_ref[...] + gv_ref[...].astype(F32)).astype(BF16)
        kv_ref[:, :HD] = dkr
        kv_ref[:, HD:] = dvr
        other = joined(sc, part_ref[...], sib_ref[...])
        first, second = in_order(sc, tensor_at, own_ref[...], other)
        half = first.shape[1]
        d_h = nt(dq_ref[:, :half], first) + nt(dq_ref[:, half:], second) + nt(dkr, wk_ref[...]) + nt(dvr, wv_ref[...])
        v = x_ref[...].astype(F32)
        r0 = inv_rms(v)
        sum_ref[...] += jnp.sum(d_h * v * r0, axis=0, keepdims=True)
        out_ref[...] = dm_ref[...].astype(F32) + pull_v(v, r0, one(gain_ref, ATTN_IN), d_h)

    wide = pl.BlockSpec((step, width), lambda i, s: (i, 0))
    mine = pl.BlockSpec((step, width), lambda i, s: (m * steps + i, 0))
    head = pl.BlockSpec((step, HD), lambda i, s: (i, 0))
    table = pl.BlockSpec((step, HD // 2), lambda i, s: (i, 0))
    return call(
        body,
        (steps,),
        [mine, wide, pl.BlockSpec((step, dq.shape[1]), lambda i, s: (i, 0)), head, head, head,
         pl.BlockSpec((step, HD), lambda i, s: (i, 1)),
         pl.BlockSpec((step, HD), lambda i, s: (m * steps + i, 0)), whole(head_gains), table, table,
         *[whole(w) for w in wq], whole(wk), whole(wv), whole(gains), *[whole(p) for p in prior]],
        [
            (x.shape, F32, mine),
            ((rows, 2 * HD), BF16, pl.BlockSpec((step, 2 * HD), lambda i, s: (i, 0))),
            ((1, width), F32, pl.BlockSpec((1, width), lambda i, s: (0, 0))),
            ((1, HD), F32, pl.BlockSpec((1, HD), lambda i, s: (0, 0))),
        ],
        [],
        chain,
        scalars,
        x, d_mid, dq, dk, dv, got, got, raw, head_gains, cosine, sine, *wq, wk, wv, gains, *prior,
        into={} if grad is None else {0: grad},
    )


def weight_gradient(chain, scalars, lefts, rights, n, tile, tiles, chunk, right_at, out_at, out_tiles, into=None, extra=None):
    width = lefts[0][0].shape[1]
    rows = WINDOW
    rps = width // n
    count = len(lefts)

    def body(sc, *refs):
        l_refs, r_refs = refs[:count], refs[count:2 * count]
        send_ref, keep_ref, left_t = refs[-3:]

        @pl.when(pl.program_id(0) == 0)
        def _():
            for k in range(count):
                left_t[:, k * rows:(k + 1) * rows] = l_refs[k][...].T

        even = sc[1] == 0
        if extra is not None:
            filled = jnp.zeros((128 - extra.shape[0], width), F32)
            more_t = jnp.concatenate([refs[2 * count][...], filled], 0).T
        for c in range(width // chunk):
            v = nn(left_t[c * chunk:(c + 1) * chunk, :rows], r_refs[0][...])
            for k in range(1, count):
                v += nn(left_t[c * chunk:(c + 1) * chunk, k * rows:(k + 1) * rows], r_refs[k][...])
            if extra is not None:
                v = jnp.concatenate([v, more_t[c * chunk:(c + 1) * chunk]], 1)
            for j in range(chunk // (2 * rps)):
                a = v[2 * j * rps:(2 * j + 1) * rps]
                b = v[(2 * j + 1) * rps:(2 * j + 2) * rps]
                at = c * (chunk // (2 * rps)) + j
                send_ref[at] = jnp.where(even, b, a).astype(BF16)
                keep_ref[at] = jnp.where(even, a, b).astype(BF16)

    more = 0 if extra is None else 128
    out = pl.BlockSpec((n // 2, rps, tile + more), lambda i, s: (0, 0, out_at + i))
    shape = (n // 2, rps, out_tiles * tile + more)

    def left_spec(at):
        return pl.BlockSpec((rows, width), lambda i, s: (at, 0))

    def right_spec(at):
        return pl.BlockSpec((rows, tile), lambda i, s: (at, right_at(s) + i))

    return call(
        body,
        (tiles,),
        [left_spec(at) for _, at in lefts] + [right_spec(at) for _, at in rights]
        + ([] if extra is None else [whole(extra)]),
        [(shape, BF16, out), (shape, BF16, out)],
        [pltpu.VMEM((width, count * rows), BF16)],
        chain,
        scalars,
        *[l for l, _ in lefts], *[r for r, _ in rights], *([] if extra is None else [extra]),
        into=None if into is None else {0: into[0], 1: into[1]},
    )


def plain_gradient(lefts, rights, n, tile, tiles, start, extra=None):
    width = lefts[0][0].shape[1]
    total = 0.0
    for (left, la), (right, ra) in zip(lefts, rights):
        left = left[la * WINDOW:(la + 1) * WINDOW]
        right = lax.dynamic_slice_in_dim(right[ra * WINDOW:(ra + 1) * WINDOW], start * tile, tile * tiles, 1)
        total = total + lax.dot_general(left, right, (((0,), (0,)), ((), ())), preferred_element_type=F32)
    if extra is not None:
        total = jnp.concatenate([total, jnp.pad(extra.T, ((0, 0), (0, 120)))], 1)
    both = total.astype(BF16).reshape(n // 2, 2, width // n, -1)
    core = my_bit(0)
    return (
        lax.dynamic_index_in_dim(both, 1 - core, 1, keepdims=False),
        lax.dynamic_index_in_dim(both, core, 1, keepdims=False),
    )


class Halving:
    def __init__(self, chain, at, send, keep, order):
        self.chain = chain
        self.at = at
        self.sum = None
        self.bits = list(range(1, lax.axis_size("dp").bit_length() - 1))[::-1]
        self.order = list(order)
        shape = (2,) * len(self.bits) + keep.shape[1:]
        self.parts = [(keep.reshape(shape), self.bits), (chain.moved(swap_dp(send, 0)).reshape(shape), self.bits)]

    def job(self):
        bit = self.order.pop(0) if self.order else None
        self.bits = [b for b in self.bits if b != bit]
        rps, columns = self.parts[0][0].shape[-2:]
        bits, at = self.bits if bit is not None else [], self.at

        def block_at(p_bits, tile):
            def index(j, s):
                def value(b):
                    mine = (s[at] >> b) & 1
                    return 1 - mine if b == bit else mine

                return tuple(0 if b in bits else value(b) for b in p_bits) + (0, j)

            return pl.BlockSpec(tuple(2 if b in bits else None for b in p_bits) + (rps, tile), index)

        def done(out):
            if bit is None:
                self.sum = out
            else:
                self.parts.append((self.chain.moved(swap_dp(out, bit)), bits))

        dtype = F32 if bit is None else BF16
        shape = (2,) * len(bits) + (rps, columns)
        return self.parts[:], block_at, shape, dtype, done


def add_parts(chain, scalars, *halvings, handed=None):
    jobs = [h.job() for h in halvings]
    steps = 1 if all(j[2][-1] % 384 == 0 for j in jobs) else 1
    ins, outs, args = [], [], []
    for parts, block_at, shape, dtype, _ in jobs:
        tile = shape[-1] // steps
        lead = shape[:-2]
        args += [p for p, _ in parts]
        ins += [block_at(bits, tile) for _, bits in parts]
        spec = pl.BlockSpec(shape[:-1] + (tile,), lambda j, s, z=(0,) * (len(lead) + 1): z + (j,))
        outs.append((shape, dtype, spec))

    more = {}
    if handed is not None:
        outs.insert(0, (handed.shape, handed.dtype, pl.BlockSpec(memory_space=pl.ANY)))
        more = dict(into={0: handed}, ahead=chain.received)

    def body(sc, *refs):
        left = refs[:len(args)]
        for (parts, _, _, dtype, _), out in zip(jobs, refs[len(refs) - len(jobs):]):
            total = left[0][...].astype(F32)
            for r in left[1:len(parts)]:
                total += r[...].astype(F32)
            out[...] = total.astype(dtype)
            left = left[len(parts):]

    results = call(body, (steps,), ins, outs, [], chain, scalars, *args, **more)
    if handed is not None:
        handed, *results = results
    for (_, _, _, _, done), out in zip(jobs, results):
        done(out)
    return handed


def shards(
    tokens,
    image_starts,
    g_attn_in,
    w_query,
    w_key,
    w_value,
    g_query,
    g_key,
    w_out,
    g_attn_post,
    g_ffn_in,
    w_gate,
    w_up,
    w_down,
    g_ffn_post,
    cotangent,
):
    mb, rows, width = tokens.shape
    own = w_query.shape[1]
    y = lax.axis_index("tensor")
    dp = lax.axis_index("dp")
    n = lax.axis_size("dp")
    offset = dp % (SEQ_LEN // rows) * rows
    cosine, sine = angle_tables(offset + jnp.arange(rows, dtype=jnp.int32))
    core = my_bit(0)
    scalars = jnp.concatenate([jnp.stack([offset, core]), image_starts[:, 0], jnp.stack([y, dp])]).astype(jnp.int32)
    low_first = list(range(1, n.bit_length() - 1))
    low_last = low_first[1:] + low_first[:1]

    x = tokens.reshape(mb * rows, width)
    cot = cotangent.reshape(mb * rows, width)
    chain = Chain()

    gains = jnp.stack([g_attn_in, g_attn_post, g_ffn_in, g_ffn_post])
    head_gains = jnp.stack([g_query, g_key])
    tensor_at = 2 + mb
    part_q = chain.moved(swap_y(pick(w_query.reshape(2, width // 2, own), core)))
    h1, key_raw, kv = pre_attention(
        chain, scalars, x, gains, w_key, w_value, head_gains, cosine, sine, rows
    )
    near = chain.moved(shift_dp(kv, 1))
    sibling_q = chain.moved(swap_dp(after(part_q, kv), 0))
    part_o = chain.moved(swap_y(pick(after(w_out, part_q).reshape(2, own // 2, width), core)))
    pair = None
    for other in (None, (part_q, sibling_q)):
        pair = queries(
            chain, scalars, tensor_at, h1, w_query, other, head_gains, cosine, sine, rows, pair
        )
    query_raw, query = pair
    mixed = attention(chain, scalars, query, near, kv, rows)
    sibling_o = chain.moved(swap_dp(after(part_o, mixed), 0))
    other_o = (part_o, sibling_o)
    branch, middle, h2 = post_attention(
        chain, scalars, tensor_at, x, mixed, w_out, *other_o, gains, rows
    )

    forward = []
    for m in range(mb):
        act, dact, hidden, part = ffn_forward(chain, scalars, m, h2, w_gate, w_up, w_down, rows, 1152, 256)
        forward.append((act, dact, hidden, part, chain.moved(swap_y(part))))

    split = width // n % 8 == 0
    hidden_width = w_gate.shape[1]

    def gradient(lefts, rights, tile, tiles, first=0, own_tile=False, out_at=0, out_tiles=None, into=None, extra=None):
        if split:
            right_at = (lambda s: s[tensor_at]) if own_tile else (lambda s: first)
            return weight_gradient(
                chain, scalars, lefts, rights, n, tile, tiles, 576, right_at, out_at, out_tiles or tiles, into, extra
            )
        made = plain_gradient(lefts, rights, n, tile, tiles, y if own_tile else first, extra)
        if into is None:
            return made
        return tuple(jnp.concatenate(p, -1) for p in zip(into, made))

    def batches(a):
        return [(a, m) for m in range(mb)]

    def each(arrays):
        return [(a, 0) for a in arrays]

    def halving(pair, order):
        return Halving(chain, 3 + mb, *pair, order)

    def serve(*halvings, handed=None):
        for h in halvings[:-1]:
            add_parts(chain, scalars, h)
        return add_parts(chain, scalars, halvings[-1], handed=handed)

    output = None
    d_ffns, grads, parts = [], [], []
    post_sum = ()
    hiddens = each([f[2] for f in forward])
    for m in range(mb):
        act, dact, hidden, part, got = forward[m]
        output, d_ffn, *post_sum = finish_forward(
            chain, scalars, m, part, got, middle, cot, gains, rows // 2, output, post_sum
        )
        d_ffns.append(d_ffn)
        if m == mb - 1:
            down = halving(gradient(each(d_ffns), hiddens, 1152, 3), low_last)
        d_gate, d_up, dh = ffn_backward(chain, scalars, d_ffn, act, dact, w_gate, w_up, w_down, 1152, 512)
        grads.append((d_gate, d_up))
        parts.append((dh, chain.moved(swap_y(dh))))

    serve(down)
    gate = halving(gradient(batches(h2), each([g[0] for g in grads]), 1152, 3), low_first)
    up = halving(gradient(batches(h2), each([g[1] for g in grads]), 1152, 3), low_first)
    serve(gate)
    chain.before_next(parts[1][1])

    back = []
    shifted = []
    for m in range(mb):
        back.append(
            attention_backward(
                chain, scalars, m, tensor_at, *parts[m], middle, cot, branch, gains, w_out, *other_o, query,
                query_raw, head_gains, cosine, sine, near, kv, back[-1][6:] if back else (),
            )
        )
        shifted.append(chain.moved(shift_dp(back[m][3], -1)))
        if m == 0:
            serve(down)
    serve(up)
    chain.before_next(shifted[0])
    own_at = dict(own_tile=True, out_tiles=2)
    pair = gradient(each([b[1] for b in back]), batches(mixed), own, 1, **own_at)
    pair = gradient(batches(h1), each([b[2] for b in back]), own, 1, out_at=1, into=pair, **own_at)
    attn = halving(pair, low_first)
    serve(gate)

    grad_input = None
    kvs = []
    in_sums = ()
    for m in range(mb):
        d_mid, d_branch, dq, _, dk, dv = back[m][:6]
        grad_input, dkv, *in_sums = input_gradient(
            chain, scalars, m, tensor_at, x, d_mid, dq, dk, dv, shifted[m], key_raw, head_gains, cosine, sine,
            (w_query, part_q, sibling_q), w_key, w_value, gains, rows // 2, grad_input, in_sums,
        )
        kvs.append(dkv)
        if m == 0:
            serve(attn)
    serve(up, gate, down)

    rps = width // n
    hps = HD // n

    def spread(sums):
        return jnp.pad(sums.reshape(n, hps), ((0, 0), (0, rps - hps))).reshape(1, width)

    extra = jnp.concatenate(
        [
            in_sums[0],
            post_sum[0],
            back[-1][6],
            back[-1][7],
            spread(back[-1][8]),
            spread(in_sums[1]),
            jnp.zeros((2, width), F32),
        ]
    )
    last = halving(gradient(batches(h1), each(kvs), 2 * HD, 1, extra=extra), low_first)
    serve(attn, last, up, down, last, attn, gate, last)
    every = (attn, down, gate, up, last)
    while last.order:
        serve(*[h for h in every if h.order])
    output = serve(*[h for h in every if h.sum is None], handed=output)
    last, grad_attn = last.sum, attn.sum
    gain_grads = last[:, 2 * HD:]
    return (
        output.reshape(tokens.shape),
        grad_input.reshape(tokens.shape),
        gain_grads[:, 0],
        grad_attn[:, own:],
        last[:, :HD],
        last[:, HD:2 * HD],
        gain_grads[:hps, 4],
        gain_grads[:hps, 5],
        grad_attn[:, :own].T,
        gain_grads[:, 3],
        gain_grads[:, 2],
        gate.sum,
        up.sum,
        down.sum.T,
        gain_grads[:, 1],
    )


def solution(mesh):
    rows = P(None, "dp", None)
    in_specs = (
        rows,
        P(None, "dp"),
        P(),
        P(None, "tensor"),
        P(),
        P(),
        P(),
        P(),
        P("tensor", None),
        P(),
        P(),
        P(None, "tensor"),
        P(None, "tensor"),
        P("tensor", None),
        P(),
        rows,
    )
    out_specs = (
        rows,
        rows,
        P("dp"),
        P("dp", "tensor"),
        P("dp", None),
        P("dp", None),
        P("dp"),
        P("dp"),
        P("tensor", "dp"),
        P("dp"),
        P("dp"),
        P("dp", "tensor"),
        P("dp", "tensor"),
        P("tensor", "dp"),
        P("dp"),
    )
    return jax.shard_map(shards, mesh=mesh, in_specs=in_specs, out_specs=out_specs, check_vma=False)
```

```python
import jax
import jax.numpy as jnp
from jax import lax
from jax.experimental import pallas as pl
from jax.experimental.pallas import tpu as pltpu
from jax.sharding import PartitionSpec as P
import numpy as np

HD = 256
WINDOW = 512
IMG = 256
SEQ_LEN = 4096
EPSILON = 1e-06
NEGATIVE = -1e30
SCALE = HD ** -0.5
GELU_C = 0.7978845608028654
GELU_A = 0.044715
F32 = jnp.float32
BF16 = jnp.bfloat16
VMEM_BYTES = 60 * 2**20
ATTN_IN, ATTN_POST, FFN_IN, FFN_POST = range(4)
QUERY, KEY = range(2)


def nn(a, b):
    return jnp.dot(a, b, preferred_element_type=F32)


def nt(a, b):
    return lax.dot_general(a, b, (((1,), (1,)), ((), ())), preferred_element_type=F32)


def inv_rms(v):
    return lax.rsqrt(jnp.mean(v * v, axis=-1, keepdims=True) + EPSILON)


def pull_v(v, r, g, e):
    eg = e * g
    return r * eg - v * (r * r * r * jnp.mean(v * eg, axis=-1, keepdims=True))


def rotate(v, cosine, sine):
    half = v.shape[-1] // 2
    a, b = v[:, :half], v[:, half:]
    return jnp.concatenate([a * cosine - b * sine, b * cosine + a * sine], axis=-1)


def rotate_back(v, cosine, sine):
    half = v.shape[-1] // 2
    a, b = v[:, :half], v[:, half:]
    return jnp.concatenate([a * cosine + b * sine, b * cosine - a * sine], axis=-1)


def angle_tables(places):
    half = HD // 2
    frequency = (10000.0 ** (-2.0 * np.arange(half) / HD)).astype(np.float32)
    angles = places.astype(F32)[:, None] * frequency[None, :]
    return jnp.cos(angles), jnp.sin(angles)


def swap_y(v):
    return lax.ppermute(v, "tensor", [(0, 1), (1, 0)])


def swap_dp(v, bit):
    n = lax.axis_size("dp")
    return lax.ppermute(v, "dp", [(i, i ^ (1 << bit)) for i in range(n)])


def shift_dp(v, steps):
    n = lax.axis_size("dp")
    first, last = max(0, -steps), min(n, n - steps)
    return lax.ppermute(v, "dp", [(i, i + steps) for i in range(first, last)])


def my_bit(bit):
    return (lax.axis_index("dp") >> bit) & 1


def after(value, *earlier):
    return lax.optimization_barrier((value,) + earlier)[0]


def pick(a, i):
    return lax.dynamic_index_in_dim(a, i, 0, keepdims=False)


class Chain:
    def __init__(self):
        self.last = ()
        self.first = []
        self.received = []

    def before_next(self, *arrays):
        self.first.extend(arrays)

    def moved(self, array):
        self.received.append(array)
        return array

    def take(self):
        taken, self.first = list(self.last) + self.first, []
        return taken


def call(body, grid, ins, outs, scratch, chain, scalars, *args, into=None, ahead=()):
    count = len(ins)
    ahead = list(ahead)
    skip = len(ahead)
    into = into or {}
    given = list(into.values())
    extra = given + [a for a in chain.take() if not any(a is g for g in given)]
    aliases = {1 + skip + count + k: out for k, out in enumerate(into)}

    anywhere = pl.BlockSpec(memory_space=pl.ANY)

    def inner(sc, *refs):
        body(sc, *refs[skip:skip + count], *refs[skip + count + len(extra):])

    results = pl.pallas_call(
        inner,
        grid_spec=pltpu.PrefetchScalarGridSpec(
            num_scalar_prefetch=1,
            grid=grid,
            in_specs=[anywhere] * skip + list(ins) + [anywhere] * len(extra),
            out_specs=[o[2] for o in outs],
            scratch_shapes=scratch,
        ),
        out_shape=[jax.ShapeDtypeStruct(s, d) for s, d, _ in outs],
        input_output_aliases=aliases,
        compiler_params=pltpu.CompilerParams(
            vmem_limit_bytes=VMEM_BYTES,
            dimension_semantics=("arbitrary",) * len(grid),
        ),
        cost_estimate=pl.CostEstimate(flops=10**14, bytes_accessed=1000, transcendentals=0),
    )(scalars, *ahead, *args, *extra)
    chain.last = (min(results, key=lambda r: r.size),)
    return results


def begin(prior, *sums):
    for k, s in enumerate(sums):
        s[...] = prior[k][...] if prior else jnp.zeros_like(s)


def one(ref, k):
    return ref[k:k + 1, :]


def whole(a):
    nd = len(a.shape)
    return pl.BlockSpec(a.shape, lambda *i: (0,) * nd)


def in_order(sc, at, own, other):
    first = sc[at] == 0
    return jnp.where(first, own, other), jnp.where(first, other, own)


def joined(sc, part, sibling):
    first = sc[1] == 0
    return jnp.concatenate([jnp.where(first, part, sibling), jnp.where(first, sibling, part)], 0)


def pre_attention(chain, scalars, x, gain, wk, wv, g_key, cosine, sine, step):
    total, width = x.shape
    rows = cosine.shape[0]

    def body(sc, x_ref, g_ref, wk_ref, wv_ref, gk_ref, cos_ref, sin_ref, h_ref, raw_ref, kv_ref):
        v = x_ref[...].astype(F32)
        h = (v * inv_rms(v) * one(g_ref, ATTN_IN)).astype(BF16)
        h_ref[...] = h
        raw = nn(h, wk_ref[...])
        raw_ref[...] = raw
        key = rotate(raw * inv_rms(raw) * one(gk_ref, KEY), cos_ref[...], sin_ref[...])
        kv_ref[:, :HD] = key.astype(BF16)
        kv_ref[:, HD:] = nn(h, wv_ref[...]).astype(BF16)

    per = rows // step
    table = pl.BlockSpec((step, HD // 2), lambda i, s: (i % per, 0))
    wide = pl.BlockSpec((step, width), lambda i, s: (i, 0))
    head = pl.BlockSpec((step, HD), lambda i, s: (i, 0))
    return call(
        body,
        (total // step,),
        [wide, whole(gain), whole(wk), whole(wv), whole(g_key), table, table],
        [
            ((total, width), BF16, wide),
            ((total, HD), F32, head),
            ((total, 2 * HD), BF16, pl.BlockSpec((step, 2 * HD), lambda i, s: (i, 0))),
        ],
        [],
        chain,
        scalars,
        x, gain, wk, wv, g_key, cosine, sine,
    )


def set_bias(sc, m, near_ref, own_ref, transposed):
    rows = near_ref.shape[0]
    q_dim, k_dim = (1, 0) if transposed else (0, 1)
    q = lax.broadcasted_iota(jnp.int32, (rows, rows), q_dim)
    k = lax.broadcasted_iota(jnp.int32, (rows, rows), k_dim)
    start = sc[2 + m]
    after = (k > q) & (sc[0] > 0)
    near_ref[...] = jnp.where(after, 0.0, NEGATIVE)
    in_q = (q >= start) & (q < start + IMG)
    in_k = (k >= start) & (k < start + IMG)
    own_ref[...] = jnp.where((k <= q) | (in_q & in_k), 0.0, NEGATIVE)


def queries(chain, scalars, at, h1, own, other, gains, cosine, sine, step, into):
    total, width = h1.shape
    columns = own.shape[1]
    weights = [own] if other is None else list(other)

    def body(sc, h_ref, *refs):
        w_refs = refs[:len(weights)]
        g_ref, cos_ref, sin_ref, raw_ref, q_ref = refs[len(weights):]
        w = w_refs[0][...] if other is None else joined(sc, w_refs[0][...], w_refs[1][...])
        both = nn(h_ref[...], w)
        raw_ref[...] = both.astype(BF16)
        for k in range(columns // HD):
            raw = both[:, k * HD:(k + 1) * HD]
            q = rotate(raw * inv_rms(raw) * one(g_ref, QUERY), cos_ref[...], sin_ref[...]) * SCALE
            q_ref[:, k * HD:(k + 1) * HD] = q.astype(BF16)

    per = cosine.shape[0] // step
    table = pl.BlockSpec((step, HD // 2), lambda i, s: (i % per, 0))
    out = pl.BlockSpec((step, columns), lambda i, s: (i, s[at] if other is None else 1 - s[at]))
    shape = (total, 2 * columns)
    return call(
        body,
        (total // step,),
        [pl.BlockSpec((step, width), lambda i, s: (i, 0))] + [whole(w) for w in weights]
        + [whole(gains), table, table],
        [(shape, BF16, out)] * 2,
        [],
        chain,
        scalars,
        h1, *weights, gains, cosine, sine,
        into={} if into is None else {0: into[0], 1: into[1]},
    )


def attention(chain, scalars, query, near, kv, rows):
    total = query.shape[0]
    heads = query.shape[1] // HD

    def body(sc, q_ref, nk_ref, k_ref, nv_ref, v_ref, mix_ref, near_bias, own_bias):
        @pl.when(pl.program_id(1) == 0)
        def _():
            set_bias(sc, pl.program_id(0), near_bias, own_bias, False)

        q = q_ref[...]
        near = jnp.exp(nt(q, nk_ref[...]) + near_bias[...])
        own = jnp.exp(nt(q, k_ref[...]) + own_bias[...])
        sums = jnp.sum(near, axis=-1, keepdims=True) + jnp.sum(own, axis=-1, keepdims=True)
        mix = nn(near.astype(BF16), nv_ref[...]) + nn(own.astype(BF16), v_ref[...])
        mix_ref[...] = (mix / sums).astype(BF16)

    key_at = pl.BlockSpec((rows, HD), lambda m, h, s: (m, 0))
    value_at = pl.BlockSpec((rows, HD), lambda m, h, s: (m, 1))
    out = pl.BlockSpec((rows, HD), lambda m, h, s: (m, h))
    return call(
        body,
        (total // rows, heads),
        [out, key_at, key_at, value_at, value_at],
        [(query.shape, BF16, out)],
        [pltpu.VMEM((rows, rows), F32)] * 2,
        chain,
        scalars,
        query, near, kv, near, kv,
    )[0]


def post_attention(chain, scalars, tensor_at, x, mixed, own, part, sibling, gains, step):
    total, width = x.shape

    def body(sc, x_ref, m_ref, own_ref, part_ref, sib_ref, g_ref, br_ref, mid_ref, h_ref):
        other = joined(sc, part_ref[...], sib_ref[...])
        first, second = in_order(sc, tensor_at, own_ref[...], other)
        branch = nn(m_ref[:, :half], first) + nn(m_ref[:, half:], second)
        br_ref[...] = branch.astype(BF16)
        middle = x_ref[...].astype(F32) + branch * inv_rms(branch) * one(g_ref, ATTN_POST)
        mid_ref[...] = middle.astype(BF16)
        h_ref[...] = (middle * inv_rms(middle) * one(g_ref, FFN_IN)).astype(BF16)

    half = own.shape[0]
    wide = pl.BlockSpec((step, width), lambda i, s: (i, 0))
    shape = (total, width)
    return call(
        body,
        (total // step,),
        [wide, pl.BlockSpec((step, mixed.shape[1]), lambda i, s: (i, 0)), whole(own), whole(part), whole(sibling), whole(gains)],
        [(shape, BF16, wide)] * 3,
        [],
        chain,
        scalars,
        x, mixed, own, part, sibling, gains,
    )


def ffn_forward(chain, scalars, m, h2, wg, wu, wd, rows, tile, chunk):
    width, hidden = wg.shape
    steps = hidden // tile

    def body(sc, h_ref, wg_ref, wu_ref, wd_ref, act_ref, dact_ref, hid_ref, out_ref, acc):
        @pl.when(pl.program_id(0) == 0)
        def _():
            acc[...] = jnp.zeros_like(acc)

        w = jnp.concatenate([wg_ref[...], wu_ref[...]], 1)
        for r in range(rows // chunk):
            at = pl.ds(r * chunk, chunk)
            both = nn(h_ref[at, :], w)
            g, u = both[:, :tile], both[:, tile:]
            g2 = g * g
            t = jnp.tanh(g * (GELU_C + GELU_C * GELU_A * g2))
            half = 0.5 + 0.5 * t
            act = g * half
            dact = half + 0.5 * g * (1.0 - t * t) * (GELU_C + 3.0 * GELU_C * GELU_A * g2)
            act_ref[at, :] = act.astype(BF16)
            dact_ref[at, :] = (dact * u).astype(BF16)
            hid = (act * u).astype(BF16)
            hid_ref[at, :] = hid
            acc[at, :] += nn(hid, wd_ref[...])

        @pl.when(pl.program_id(0) == steps - 1)
        def _():
            out_ref[...] = acc[...].astype(BF16)

    col = pl.BlockSpec((width, tile), lambda i, s: (0, i))
    act = pl.BlockSpec((rows, tile), lambda i, s: (0, i))
    return call(
        body,
        (steps,),
        [pl.BlockSpec((rows, width), lambda i, s: (m, 0)), col, col, pl.BlockSpec((tile, width), lambda i, s: (i, 0))],
        [((rows, hidden), BF16, act)] * 3 + [((rows, width), BF16, pl.BlockSpec((rows, width), lambda i, s: (0, 0)))],
        [pltpu.VMEM((rows, width), F32)],
        chain,
        scalars,
        h2, wg, wu, wd,
    )


def finish_forward(chain, scalars, m, part, got, middle, cot, gain, step, output, prior):
    rows, width = part.shape
    steps = rows // step

    def body(sc, p_ref, q_ref, mid_ref, c_ref, g_ref, *refs):
        out_ref, d_ref, gain_ref = refs[-3:]

        @pl.when(pl.program_id(0) == 0)
        def _():
            begin(refs[:-3], gain_ref)

        ffn = p_ref[...].astype(F32) + q_ref[...].astype(F32)
        r3 = inv_rms(ffn)
        c = c_ref[...].astype(F32)
        n = ffn * r3
        out_ref[...] = (mid_ref[...].astype(F32) + n * one(g_ref, FFN_POST)).astype(BF16)
        d_ref[...] = pull_v(ffn, r3, one(g_ref, FFN_POST), c).astype(BF16)
        gain_ref[...] += jnp.sum(c * n, axis=0, keepdims=True)

    wide = pl.BlockSpec((step, width), lambda i, s: (i, 0))
    mine = pl.BlockSpec((step, width), lambda i, s: (m * steps + i, 0))
    return call(
        body,
        (steps,),
        [wide, wide, mine, mine, whole(gain)] + [whole(p) for p in prior],
        [
            (cot.shape, BF16, mine),
            ((rows, width), BF16, wide),
            ((1, width), F32, pl.BlockSpec((1, width), lambda i, s: (0, 0))),
        ],
        [],
        chain,
        scalars,
        part, got, middle, cot, gain, *prior,
        into={} if output is None else {0: output},
    )


def ffn_backward(chain, scalars, d_ffn, act, dact, wg, wu, wd, tile, chunk):
    width, hidden = wg.shape
    rows = d_ffn.shape[0]
    steps = hidden // tile

    def body(sc, d_ref, act_ref, dact_ref, wg_ref, wu_ref, wd_ref, dg_ref, du_ref, dh_ref, acc):
        @pl.when(pl.program_id(0) == 0)
        def _():
            acc[...] = jnp.zeros_like(acc)

        w = jnp.concatenate([wg_ref[...], wu_ref[...]], 1)
        for r in range(rows // chunk):
            at = pl.ds(r * chunk, chunk)
            dh = nt(d_ref[at, :], wd_ref[...])
            du = (dh * act_ref[at, :].astype(F32)).astype(BF16)
            dg = (dh * dact_ref[at, :].astype(F32)).astype(BF16)
            dg_ref[at, :] = dg
            du_ref[at, :] = du
            acc[at, :] += nt(jnp.concatenate([dg, du], 1), w)

        @pl.when(pl.program_id(0) == steps - 1)
        def _():
            dh_ref[...] = acc[...].astype(BF16)

    col = pl.BlockSpec((width, tile), lambda i, s: (0, i))
    acts = pl.BlockSpec((rows, tile), lambda i, s: (0, i))
    wide = pl.BlockSpec((rows, width), lambda i, s: (0, 0))
    return call(
        body,
        (steps,),
        [wide, acts, acts, col, col, pl.BlockSpec((tile, width), lambda i, s: (i, 0))],
        [((rows, hidden), BF16, acts), ((rows, hidden), BF16, acts), ((rows, width), BF16, wide)],
        [pltpu.VMEM((rows, width), F32)],
        chain,
        scalars,
        d_ffn, act, dact, wg, wu, wd,
    )


def attention_backward(chain, scalars, m, tensor_at, part, got, middle, cot, branch, gains, own, part_o, sibling_o, q, raw, head_gains,
                       cosine, sine, near, kv, prior):
    rows, width = part.shape
    per = own.shape[0] // HD
    heads = 2 * per

    def body(sc, p_ref, o_ref, mid_ref, c_ref, br_ref, g_ref, own_ref, part_ref, sib_ref, q_ref, raw_ref, gq_ref,
             cos_ref, sin_ref, nk_ref, k_ref, nv_ref, v_ref, *refs):
        (dm_ref, db_ref, dq_ref, dn_ref, dk_ref, dv_ref, sum_f_ref, sum_a_ref, sum_q_ref,
         near_bias, own_bias, near_kt, own_kt, acc) = refs[len(prior):]
        h = pl.program_id(0)

        @pl.when(h == 0)
        def _():
            set_bias(sc, m, near_bias, own_bias, True)
            near_kt[...] = nk_ref[...].T
            own_kt[...] = k_ref[...].T
            acc[...] = jnp.zeros_like(acc)
            begin(refs[:len(prior)], sum_f_ref, sum_a_ref, sum_q_ref)
            for r in range(rows // 128):
                at = pl.ds(r * 128, 128)
                e = p_ref[at, :].astype(F32) + o_ref[at, :].astype(F32)
                mid = mid_ref[at, :].astype(F32)
                r2 = inv_rms(mid)
                d_mid = c_ref[at, :].astype(F32) + pull_v(mid, r2, one(g_ref, FFN_IN), e)
                dm_ref[at, :] = d_mid.astype(BF16)
                sum_f_ref[...] += jnp.sum(e * mid * r2, axis=0, keepdims=True)
                branch = br_ref[at, :].astype(F32)
                r1 = inv_rms(branch)
                sum_a_ref[...] += jnp.sum(d_mid * branch * r1, axis=0, keepdims=True)
                db_ref[at, :] = pull_v(branch, r1, one(g_ref, ATTN_POST), d_mid).astype(BF16)

        other = jnp.where(h % per == sc[1], part_ref[...], sib_ref[...])
        wo = jnp.where(h // per == sc[tensor_at], own_ref[...], other)
        d_mix = nt(db_ref[...], wo).astype(BF16)
        qv = q_ref[...]
        near = jnp.exp(nt(nk_ref[...], qv) + near_bias[...])
        own = jnp.exp(nt(k_ref[...], qv) + own_bias[...])
        inv = 1.0 / (jnp.sum(near, axis=0, keepdims=True) + jnp.sum(own, axis=0, keepdims=True))
        near = near * inv
        own = own * inv
        acc[2] += nn(near.astype(BF16), d_mix)
        acc[3] += nn(own.astype(BF16), d_mix)
        dp_near = nt(nv_ref[...], d_mix)
        dp_own = nt(v_ref[...], d_mix)
        dots = jnp.sum(near * dp_near, axis=0, keepdims=True) + jnp.sum(own * dp_own, axis=0, keepdims=True)
        ds_near = (near * (dp_near - dots)).astype(BF16)
        ds_own = (own * (dp_own - dots)).astype(BF16)
        acc[0] += nn(ds_near, qv)
        acc[1] += nn(ds_own, qv)
        d_q = (nn(near_kt[...], ds_near) + nn(own_kt[...], ds_own)).T
        e_q = rotate_back(d_q * SCALE, cos_ref[...], sin_ref[...])
        raw_v = raw_ref[...].astype(F32)
        rq = inv_rms(raw_v)
        sum_q_ref[...] += jnp.sum(e_q * raw_v * rq, axis=0, keepdims=True)
        dq_ref[...] = pull_v(raw_v, rq, one(gq_ref, QUERY), e_q).astype(BF16)

        @pl.when(h == heads - 1)
        def _():
            dn_ref[:, :HD] = acc[0].astype(BF16)
            dk_ref[...] = acc[1]
            dn_ref[:, HD:] = acc[2].astype(BF16)
            dv_ref[...] = acc[3]

    wide = pl.BlockSpec((rows, width), lambda h, s: (0, 0))
    mine = pl.BlockSpec((rows, width), lambda h, s: (m, 0))
    key_at = pl.BlockSpec((rows, HD), lambda h, s: (m, 0))
    value_at = pl.BlockSpec((rows, HD), lambda h, s: (m, 1))
    heads_at = pl.BlockSpec((rows, HD), lambda h, s: (m, h))
    small = pl.BlockSpec((rows, HD), lambda h, s: (0, 0))
    sums = pl.BlockSpec((1, width), lambda h, s: (0, 0))
    weight = pl.BlockSpec((HD, width), lambda h, s: (h % per, 0))
    return call(
        body,
        (heads,),
        [wide, wide, mine, mine, mine, whole(gains), weight, whole(part_o), whole(sibling_o), heads_at, heads_at, whole(head_gains), whole(cosine), whole(sine),
         key_at, key_at, value_at, value_at] + [whole(p) for p in prior],
        [
            ((rows, width), BF16, wide),
            ((rows, width), BF16, wide),
            ((rows, heads * HD), BF16, pl.BlockSpec((rows, HD), lambda h, s: (0, h))),
            ((rows, 2 * HD), BF16, pl.BlockSpec((rows, 2 * HD), lambda h, s: (0, 0))),
            ((rows, HD), F32, small),
            ((rows, HD), F32, small),
            ((1, width), F32, sums),
            ((1, width), F32, sums),
            ((1, HD), F32, pl.BlockSpec((1, HD), lambda h, s: (0, 0))),
        ],
        [pltpu.VMEM((rows, rows), F32)] * 2 + [pltpu.VMEM((HD, rows), BF16)] * 2 + [pltpu.VMEM((4, rows, HD), F32)],
        chain,
        scalars,
        part, got, middle, cot, branch, gains, own, part_o, sibling_o, q, raw, head_gains, cosine, sine,
        near, kv, near, kv, *prior,
    )


def input_gradient(chain, scalars, m, tensor_at, x, d_mid, dq, dk, dv, got, raw, head_gains, cosine, sine, wq, wk, wv, gains, step, grad, prior):
    rows, width = d_mid.shape
    steps = rows // step

    def body(sc, x_ref, dm_ref, dq_ref, dk_ref, dv_ref, gk_ref, gv_ref, raw_ref, g_ref, cos_ref, sin_ref,
             own_ref, part_ref, sib_ref, wk_ref, wv_ref, gain_ref, *refs):
        out_ref, kv_ref, sum_ref, sum_k_ref = refs[-4:]

        @pl.when(pl.program_id(0) == 0)
        def _():
            begin(refs[:-4], sum_ref, sum_k_ref)

        e = rotate_back(dk_ref[...] + gk_ref[...].astype(F32), cos_ref[...], sin_ref[...])
        raw_v = raw_ref[...]
        rk = inv_rms(raw_v)
        sum_k_ref[...] += jnp.sum(e * raw_v * rk, axis=0, keepdims=True)
        dkr = pull_v(raw_v, rk, one(g_ref, KEY), e).astype(BF16)
        dvr = (dv_ref[...] + gv_ref[...].astype(F32)).astype(BF16)
        kv_ref[:, :HD] = dkr
        kv_ref[:, HD:] = dvr
        other = joined(sc, part_ref[...], sib_ref[...])
        first, second = in_order(sc, tensor_at, own_ref[...], other)
        half = first.shape[1]
        d_h = nt(dq_ref[:, :half], first) + nt(dq_ref[:, half:], second) + nt(dkr, wk_ref[...]) + nt(dvr, wv_ref[...])
        v = x_ref[...].astype(F32)
        r0 = inv_rms(v)
        sum_ref[...] += jnp.sum(d_h * v * r0, axis=0, keepdims=True)
        out_ref[...] = dm_ref[...].astype(F32) + pull_v(v, r0, one(gain_ref, ATTN_IN), d_h)

    wide = pl.BlockSpec((step, width), lambda i, s: (i, 0))
    mine = pl.BlockSpec((step, width), lambda i, s: (m * steps + i, 0))
    head = pl.BlockSpec((step, HD), lambda i, s: (i, 0))
    table = pl.BlockSpec((step, HD // 2), lambda i, s: (i, 0))
    return call(
        body,
        (steps,),
        [mine, wide, pl.BlockSpec((step, dq.shape[1]), lambda i, s: (i, 0)), head, head, head,
         pl.BlockSpec((step, HD), lambda i, s: (i, 1)),
         pl.BlockSpec((step, HD), lambda i, s: (m * steps + i, 0)), whole(head_gains), table, table,
         *[whole(w) for w in wq], whole(wk), whole(wv), whole(gains), *[whole(p) for p in prior]],
        [
            (x.shape, F32, mine),
            ((rows, 2 * HD), BF16, pl.BlockSpec((step, 2 * HD), lambda i, s: (i, 0))),
            ((1, width), F32, pl.BlockSpec((1, width), lambda i, s: (0, 0))),
            ((1, HD), F32, pl.BlockSpec((1, HD), lambda i, s: (0, 0))),
        ],
        [],
        chain,
        scalars,
        x, d_mid, dq, dk, dv, got, got, raw, head_gains, cosine, sine, *wq, wk, wv, gains, *prior,
        into={} if grad is None else {0: grad},
    )


def weight_gradient(chain, scalars, lefts, rights, n, tile, tiles, chunk, right_at, out_at, out_tiles, into=None, extra=None):
    width = lefts[0][0].shape[1]
    rows = WINDOW
    rps = width // n
    count = len(lefts)

    def body(sc, *refs):
        l_refs, r_refs = refs[:count], refs[count:2 * count]
        send_ref, keep_ref, left_t = refs[-3:]

        @pl.when(pl.program_id(0) == 0)
        def _():
            for k in range(count):
                left_t[:, k * rows:(k + 1) * rows] = l_refs[k][...].T

        even = sc[1] == 0
        if extra is not None:
            filled = jnp.zeros((128 - extra.shape[0], width), F32)
            more_t = jnp.concatenate([refs[2 * count][...], filled], 0).T
        for c in range(width // chunk):
            v = nn(left_t[c * chunk:(c + 1) * chunk, :rows], r_refs[0][...])
            for k in range(1, count):
                v += nn(left_t[c * chunk:(c + 1) * chunk, k * rows:(k + 1) * rows], r_refs[k][...])
            if extra is not None:
                v = jnp.concatenate([v, more_t[c * chunk:(c + 1) * chunk]], 1)
            for j in range(chunk // (2 * rps)):
                a = v[2 * j * rps:(2 * j + 1) * rps]
                b = v[(2 * j + 1) * rps:(2 * j + 2) * rps]
                at = c * (chunk // (2 * rps)) + j
                send_ref[at] = jnp.where(even, b, a).astype(BF16)
                keep_ref[at] = jnp.where(even, a, b).astype(BF16)

    more = 0 if extra is None else 128
    out = pl.BlockSpec((n // 2, rps, tile + more), lambda i, s: (0, 0, out_at + i))
    shape = (n // 2, rps, out_tiles * tile + more)

    def left_spec(at):
        return pl.BlockSpec((rows, width), lambda i, s: (at, 0))

    def right_spec(at):
        return pl.BlockSpec((rows, tile), lambda i, s: (at, right_at(s) + i))

    return call(
        body,
        (tiles,),
        [left_spec(at) for _, at in lefts] + [right_spec(at) for _, at in rights]
        + ([] if extra is None else [whole(extra)]),
        [(shape, BF16, out), (shape, BF16, out)],
        [pltpu.VMEM((width, count * rows), BF16)],
        chain,
        scalars,
        *[l for l, _ in lefts], *[r for r, _ in rights], *([] if extra is None else [extra]),
        into=None if into is None else {0: into[0], 1: into[1]},
    )


def plain_gradient(lefts, rights, n, tile, tiles, start, extra=None):
    width = lefts[0][0].shape[1]
    total = 0.0
    for (left, la), (right, ra) in zip(lefts, rights):
        left = left[la * WINDOW:(la + 1) * WINDOW]
        right = lax.dynamic_slice_in_dim(right[ra * WINDOW:(ra + 1) * WINDOW], start * tile, tile * tiles, 1)
        total = total + lax.dot_general(left, right, (((0,), (0,)), ((), ())), preferred_element_type=F32)
    if extra is not None:
        total = jnp.concatenate([total, jnp.pad(extra.T, ((0, 0), (0, 120)))], 1)
    both = total.astype(BF16).reshape(n // 2, 2, width // n, -1)
    core = my_bit(0)
    return (
        lax.dynamic_index_in_dim(both, 1 - core, 1, keepdims=False),
        lax.dynamic_index_in_dim(both, core, 1, keepdims=False),
    )


class Halving:
    def __init__(self, chain, at, send, keep, order):
        self.chain = chain
        self.at = at
        self.sum = None
        self.bits = list(range(1, lax.axis_size("dp").bit_length() - 1))[::-1]
        self.order = list(order)
        shape = (2,) * len(self.bits) + keep.shape[1:]
        self.parts = [(keep.reshape(shape), self.bits), (chain.moved(swap_dp(send, 0)).reshape(shape), self.bits)]

    def job(self):
        bit = self.order.pop(0) if self.order else None
        self.bits = [b for b in self.bits if b != bit]
        rps, columns = self.parts[0][0].shape[-2:]
        bits, at = self.bits if bit is not None else [], self.at

        def block_at(p_bits, tile):
            def index(j, s):
                def value(b):
                    mine = (s[at] >> b) & 1
                    return 1 - mine if b == bit else mine

                return tuple(0 if b in bits else value(b) for b in p_bits) + (0, j)

            return pl.BlockSpec(tuple(2 if b in bits else None for b in p_bits) + (rps, tile), index)

        def done(out):
            if bit is None:
                self.sum = out
            else:
                self.parts.append((self.chain.moved(swap_dp(out, bit)), bits))

        dtype = F32 if bit is None else BF16
        shape = (2,) * len(bits) + (rps, columns)
        return self.parts[:], block_at, shape, dtype, done


def add_parts(chain, scalars, *halvings, handed=None):
    jobs = [h.job() for h in halvings]
    steps = 1 if all(j[2][-1] % 384 == 0 for j in jobs) else 1
    ins, outs, args = [], [], []
    for parts, block_at, shape, dtype, _ in jobs:
        tile = shape[-1] // steps
        lead = shape[:-2]
        args += [p for p, _ in parts]
        ins += [block_at(bits, tile) for _, bits in parts]
        spec = pl.BlockSpec(shape[:-1] + (tile,), lambda j, s, z=(0,) * (len(lead) + 1): z + (j,))
        outs.append((shape, dtype, spec))

    more = {}
    if handed is not None:
        outs.insert(0, (handed.shape, handed.dtype, pl.BlockSpec(memory_space=pl.ANY)))
        more = dict(into={0: handed}, ahead=chain.received)

    def body(sc, *refs):
        left = refs[:len(args)]
        for (parts, _, _, dtype, _), out in zip(jobs, refs[len(refs) - len(jobs):]):
            total = left[0][...].astype(F32)
            for r in left[1:len(parts)]:
                total += r[...].astype(F32)
            out[...] = total.astype(dtype)
            left = left[len(parts):]

    results = call(body, (steps,), ins, outs, [], chain, scalars, *args, **more)
    if handed is not None:
        handed, *results = results
    for (_, _, _, _, done), out in zip(jobs, results):
        done(out)
    return handed


def shards(
    tokens,
    image_starts,
    g_attn_in,
    w_query,
    w_key,
    w_value,
    g_query,
    g_key,
    w_out,
    g_attn_post,
    g_ffn_in,
    w_gate,
    w_up,
    w_down,
    g_ffn_post,
    cotangent,
):
    mb, rows, width = tokens.shape
    own = w_query.shape[1]
    y = lax.axis_index("tensor")
    dp = lax.axis_index("dp")
    n = lax.axis_size("dp")
    offset = dp % (SEQ_LEN // rows) * rows
    cosine, sine = angle_tables(offset + jnp.arange(rows, dtype=jnp.int32))
    core = my_bit(0)
    scalars = jnp.concatenate([jnp.stack([offset, core]), image_starts[:, 0], jnp.stack([y, dp])]).astype(jnp.int32)
    low_first = list(range(1, n.bit_length() - 1))
    low_last = low_first[1:] + low_first[:1]

    x = tokens.reshape(mb * rows, width)
    cot = cotangent.reshape(mb * rows, width)
    chain = Chain()

    gains = jnp.stack([g_attn_in, g_attn_post, g_ffn_in, g_ffn_post])
    head_gains = jnp.stack([g_query, g_key])
    tensor_at = 2 + mb
    part_q = chain.moved(swap_y(pick(w_query.reshape(2, width // 2, own), core)))
    h1, key_raw, kv = pre_attention(
        chain, scalars, x, gains, w_key, w_value, head_gains, cosine, sine, rows
    )
    near = chain.moved(shift_dp(kv, 1))
    sibling_q = chain.moved(swap_dp(after(part_q, kv), 0))
    part_o = chain.moved(swap_y(pick(after(w_out, part_q).reshape(2, own // 2, width), core)))
    pair = None
    for other in (None, (part_q, sibling_q)):
        pair = queries(
            chain, scalars, tensor_at, h1, w_query, other, head_gains, cosine, sine, rows, pair
        )
    query_raw, query = pair
    mixed = attention(chain, scalars, query, near, kv, rows)
    sibling_o = chain.moved(swap_dp(after(part_o, mixed), 0))
    other_o = (part_o, sibling_o)
    branch, middle, h2 = post_attention(
        chain, scalars, tensor_at, x, mixed, w_out, *other_o, gains, rows
    )

    forward = []
    for m in range(mb):
        act, dact, hidden, part = ffn_forward(chain, scalars, m, h2, w_gate, w_up, w_down, rows, 1152, 256)
        forward.append((act, dact, hidden, part, chain.moved(swap_y(part))))

    split = width // n % 8 == 0
    hidden_width = w_gate.shape[1]

    def gradient(lefts, rights, tile, tiles, first=0, own_tile=False, out_at=0, out_tiles=None, into=None, extra=None):
        if split:
            right_at = (lambda s: s[tensor_at]) if own_tile else (lambda s: first)
            return weight_gradient(
                chain, scalars, lefts, rights, n, tile, tiles, 576, right_at, out_at, out_tiles or tiles, into, extra
            )
        made = plain_gradient(lefts, rights, n, tile, tiles, y if own_tile else first, extra)
        if into is None:
            return made
        return tuple(jnp.concatenate(p, -1) for p in zip(into, made))

    def batches(a):
        return [(a, m) for m in range(mb)]

    def each(arrays):
        return [(a, 0) for a in arrays]

    def halving(pair, order):
        return Halving(chain, 3 + mb, *pair, order)

    def serve(*halvings, handed=None):
        for h in halvings[:-1]:
            add_parts(chain, scalars, h)
        return add_parts(chain, scalars, halvings[-1], handed=handed)

    output = None
    d_ffns, grads, parts = [], [], []
    post_sum = ()
    hiddens = each([f[2] for f in forward])
    for m in range(mb):
        act, dact, hidden, part, got = forward[m]
        output, d_ffn, *post_sum = finish_forward(
            chain, scalars, m, part, got, middle, cot, gains, rows // 2, output, post_sum
        )
        d_ffns.append(d_ffn)
        if m == mb - 1:
            down = halving(gradient(each(d_ffns), hiddens, 1152, 3), low_last)
        d_gate, d_up, dh = ffn_backward(chain, scalars, d_ffn, act, dact, w_gate, w_up, w_down, 1152, 512)
        grads.append((d_gate, d_up))
        parts.append((dh, chain.moved(swap_y(dh))))

    serve(down)
    gate = halving(gradient(batches(h2), each([g[0] for g in grads]), 1152, 3), low_first)
    up = halving(gradient(batches(h2), each([g[1] for g in grads]), 1152, 3), low_first)
    serve(gate)
    chain.before_next(parts[1][1])

    back = []
    shifted = []
    for m in range(mb):
        back.append(
            attention_backward(
                chain, scalars, m, tensor_at, *parts[m], middle, cot, branch, gains, w_out, *other_o, query,
                query_raw, head_gains, cosine, sine, near, kv, back[-1][6:] if back else (),
            )
        )
        shifted.append(chain.moved(shift_dp(back[m][3], -1)))
        if m == 0:
            serve(down)
    serve(up)
    chain.before_next(shifted[0])
    own_at = dict(own_tile=True, out_tiles=2)
    pair = gradient(each([b[1] for b in back]), batches(mixed), own, 1, **own_at)
    pair = gradient(batches(h1), each([b[2] for b in back]), own, 1, out_at=1, into=pair, **own_at)
    attn = halving(pair, low_first)
    serve(gate)

    grad_input = None
    kvs = []
    in_sums = ()
    for m in range(mb):
        d_mid, d_branch, dq, _, dk, dv = back[m][:6]
        grad_input, dkv, *in_sums = input_gradient(
            chain, scalars, m, tensor_at, x, d_mid, dq, dk, dv, shifted[m], key_raw, head_gains, cosine, sine,
            (w_query, part_q, sibling_q), w_key, w_value, gains, rows // 2, grad_input, in_sums,
        )
        kvs.append(dkv)

    rps = width // n
    hps = HD // n

    def spread(sums):
        return jnp.pad(sums.reshape(n, hps), ((0, 0), (0, rps - hps))).reshape(1, width)

    extra = jnp.concatenate(
        [
            in_sums[0],
            post_sum[0],
            back[-1][6],
            back[-1][7],
            spread(back[-1][8]),
            spread(in_sums[1]),
            jnp.zeros((2, width), F32),
        ]
    )
    last = halving(gradient(batches(h1), each(kvs), 2 * HD, 1, extra=extra), low_first)
    serve(gate, up, attn, last, down, up, attn, last, gate, attn, down, last)
    every = (attn, down, gate, up, last)
    while last.order:
        serve(*[h for h in every if h.order])
    output = serve(*[h for h in every if h.sum is None], handed=output)
    last, grad_attn = last.sum, attn.sum
    gain_grads = last[:, 2 * HD:]
    return (
        output.reshape(tokens.shape),
        grad_input.reshape(tokens.shape),
        gain_grads[:, 0],
        grad_attn[:, own:],
        last[:, :HD],
        last[:, HD:2 * HD],
        gain_grads[:hps, 4],
        gain_grads[:hps, 5],
        grad_attn[:, :own].T,
        gain_grads[:, 3],
        gain_grads[:, 2],
        gate.sum,
        up.sum,
        down.sum.T,
        gain_grads[:, 1],
    )


def solution(mesh):
    rows = P(None, "dp", None)
    in_specs = (
        rows,
        P(None, "dp"),
        P(),
        P(None, "tensor"),
        P(),
        P(),
        P(),
        P(),
        P("tensor", None),
        P(),
        P(),
        P(None, "tensor"),
        P(None, "tensor"),
        P("tensor", None),
        P(),
        rows,
    )
    out_specs = (
        rows,
        rows,
        P("dp"),
        P("dp", "tensor"),
        P("dp", None),
        P("dp", None),
        P("dp"),
        P("dp"),
        P("tensor", "dp"),
        P("dp"),
        P("dp"),
        P("dp", "tensor"),
        P("dp", "tensor"),
        P("tensor", "dp"),
        P("dp"),
    )
    return jax.shard_map(shards, mesh=mesh, in_specs=in_specs, out_specs=out_specs, check_vma=False)
```

```python
import jax
import jax.numpy as jnp
from jax import lax
from jax.experimental import pallas as pl
from jax.experimental.pallas import tpu as pltpu
from jax.sharding import PartitionSpec as P
import numpy as np

HD = 256
WINDOW = 512
IMG = 256
SEQ_LEN = 4096
EPSILON = 1e-06
NEGATIVE = -1e30
SCALE = HD ** -0.5
GELU_C = 0.7978845608028654
GELU_A = 0.044715
F32 = jnp.float32
BF16 = jnp.bfloat16
VMEM_BYTES = 60 * 2**20
ATTN_IN, ATTN_POST, FFN_IN, FFN_POST = range(4)
QUERY, KEY = range(2)


def nn(a, b):
    return jnp.dot(a, b, preferred_element_type=F32)


def nt(a, b):
    return lax.dot_general(a, b, (((1,), (1,)), ((), ())), preferred_element_type=F32)


def inv_rms(v):
    return lax.rsqrt(jnp.mean(v * v, axis=-1, keepdims=True) + EPSILON)


def pull_v(v, r, g, e):
    eg = e * g
    return r * eg - v * (r * r * r * jnp.mean(v * eg, axis=-1, keepdims=True))


def rotate(v, cosine, sine):
    half = v.shape[-1] // 2
    a, b = v[:, :half], v[:, half:]
    return jnp.concatenate([a * cosine - b * sine, b * cosine + a * sine], axis=-1)


def rotate_back(v, cosine, sine):
    half = v.shape[-1] // 2
    a, b = v[:, :half], v[:, half:]
    return jnp.concatenate([a * cosine + b * sine, b * cosine - a * sine], axis=-1)


def angle_tables(places):
    half = HD // 2
    frequency = (10000.0 ** (-2.0 * np.arange(half) / HD)).astype(np.float32)
    angles = places.astype(F32)[:, None] * frequency[None, :]
    return jnp.cos(angles), jnp.sin(angles)


def swap_y(v):
    return lax.ppermute(v, "tensor", [(0, 1), (1, 0)])


def swap_dp(v, bit):
    n = lax.axis_size("dp")
    return lax.ppermute(v, "dp", [(i, i ^ (1 << bit)) for i in range(n)])


def shift_dp(v, steps):
    n = lax.axis_size("dp")
    first, last = max(0, -steps), min(n, n - steps)
    return lax.ppermute(v, "dp", [(i, i + steps) for i in range(first, last)])


def my_bit(bit):
    return (lax.axis_index("dp") >> bit) & 1


def after(value, *earlier):
    return lax.optimization_barrier((value,) + earlier)[0]


def pick(a, i):
    return lax.dynamic_index_in_dim(a, i, 0, keepdims=False)


class Chain:
    def __init__(self):
        self.last = ()
        self.first = []
        self.received = []

    def before_next(self, *arrays):
        self.first.extend(arrays)

    def moved(self, array):
        self.received.append(array)
        return array

    def take(self):
        taken, self.first = list(self.last) + self.first, []
        return taken


def call(body, grid, ins, outs, scratch, chain, scalars, *args, into=None, ahead=()):
    count = len(ins)
    ahead = list(ahead)
    skip = len(ahead)
    into = into or {}
    given = list(into.values())
    extra = given + [a for a in chain.take() if not any(a is g for g in given)]
    aliases = {1 + skip + count + k: out for k, out in enumerate(into)}

    anywhere = pl.BlockSpec(memory_space=pl.ANY)

    def inner(sc, *refs):
        body(sc, *refs[skip:skip + count], *refs[skip + count + len(extra):])

    results = pl.pallas_call(
        inner,
        grid_spec=pltpu.PrefetchScalarGridSpec(
            num_scalar_prefetch=1,
            grid=grid,
            in_specs=[anywhere] * skip + list(ins) + [anywhere] * len(extra),
            out_specs=[o[2] for o in outs],
            scratch_shapes=scratch,
        ),
        out_shape=[jax.ShapeDtypeStruct(s, d) for s, d, _ in outs],
        input_output_aliases=aliases,
        compiler_params=pltpu.CompilerParams(
            vmem_limit_bytes=VMEM_BYTES,
            dimension_semantics=("arbitrary",) * len(grid),
        ),
        cost_estimate=pl.CostEstimate(flops=10**14, bytes_accessed=1000, transcendentals=0),
    )(scalars, *ahead, *args, *extra)
    chain.last = (min(results, key=lambda r: r.size),)
    return results


def begin(prior, *sums):
    for k, s in enumerate(sums):
        s[...] = prior[k][...] if prior else jnp.zeros_like(s)


def one(ref, k):
    return ref[k:k + 1, :]


def whole(a):
    nd = len(a.shape)
    return pl.BlockSpec(a.shape, lambda *i: (0,) * nd)


def in_order(sc, at, own, other):
    first = sc[at] == 0
    return jnp.where(first, own, other), jnp.where(first, other, own)


def joined(sc, part, sibling):
    first = sc[1] == 0
    return jnp.concatenate([jnp.where(first, part, sibling), jnp.where(first, sibling, part)], 0)


def pre_attention(chain, scalars, x, gain, wk, wv, g_key, cosine, sine, step):
    total, width = x.shape
    rows = cosine.shape[0]

    def body(sc, x_ref, g_ref, wk_ref, wv_ref, gk_ref, cos_ref, sin_ref, h_ref, raw_ref, kv_ref):
        v = x_ref[...].astype(F32)
        h = (v * inv_rms(v) * one(g_ref, ATTN_IN)).astype(BF16)
        h_ref[...] = h
        raw = nn(h, wk_ref[...])
        raw_ref[...] = raw
        key = rotate(raw * inv_rms(raw) * one(gk_ref, KEY), cos_ref[...], sin_ref[...])
        kv_ref[:, :HD] = key.astype(BF16)
        kv_ref[:, HD:] = nn(h, wv_ref[...]).astype(BF16)

    per = rows // step
    table = pl.BlockSpec((step, HD // 2), lambda i, s: (i % per, 0))
    wide = pl.BlockSpec((step, width), lambda i, s: (i, 0))
    head = pl.BlockSpec((step, HD), lambda i, s: (i, 0))
    return call(
        body,
        (total // step,),
        [wide, whole(gain), whole(wk), whole(wv), whole(g_key), table, table],
        [
            ((total, width), BF16, wide),
            ((total, HD), F32, head),
            ((total, 2 * HD), BF16, pl.BlockSpec((step, 2 * HD), lambda i, s: (i, 0))),
        ],
        [],
        chain,
        scalars,
        x, gain, wk, wv, g_key, cosine, sine,
    )


def set_bias(sc, m, near_ref, own_ref, transposed):
    rows = near_ref.shape[0]
    q_dim, k_dim = (1, 0) if transposed else (0, 1)
    q = lax.broadcasted_iota(jnp.int32, (rows, rows), q_dim)
    k = lax.broadcasted_iota(jnp.int32, (rows, rows), k_dim)
    start = sc[2 + m]
    after = (k > q) & (sc[0] > 0)
    near_ref[...] = jnp.where(after, 0.0, NEGATIVE)
    in_q = (q >= start) & (q < start + IMG)
    in_k = (k >= start) & (k < start + IMG)
    own_ref[...] = jnp.where((k <= q) | (in_q & in_k), 0.0, NEGATIVE)


def queries(chain, scalars, at, h1, own, other, gains, cosine, sine, step, into):
    total, width = h1.shape
    columns = own.shape[1]
    weights = [own] if other is None else list(other)

    def body(sc, h_ref, *refs):
        w_refs = refs[:len(weights)]
        g_ref, cos_ref, sin_ref, raw_ref, q_ref = refs[len(weights):]
        w = w_refs[0][...] if other is None else joined(sc, w_refs[0][...], w_refs[1][...])
        both = nn(h_ref[...], w)
        raw_ref[...] = both.astype(BF16)
        for k in range(columns // HD):
            raw = both[:, k * HD:(k + 1) * HD]
            q = rotate(raw * inv_rms(raw) * one(g_ref, QUERY), cos_ref[...], sin_ref[...]) * SCALE
            q_ref[:, k * HD:(k + 1) * HD] = q.astype(BF16)

    per = cosine.shape[0] // step
    table = pl.BlockSpec((step, HD // 2), lambda i, s: (i % per, 0))
    out = pl.BlockSpec((step, columns), lambda i, s: (i, s[at] if other is None else 1 - s[at]))
    shape = (total, 2 * columns)
    return call(
        body,
        (total // step,),
        [pl.BlockSpec((step, width), lambda i, s: (i, 0))] + [whole(w) for w in weights]
        + [whole(gains), table, table],
        [(shape, BF16, out)] * 2,
        [],
        chain,
        scalars,
        h1, *weights, gains, cosine, sine,
        into={} if into is None else {0: into[0], 1: into[1]},
    )


def attention(chain, scalars, query, near, kv, rows):
    total = query.shape[0]
    heads = query.shape[1] // HD

    def body(sc, q_ref, nk_ref, k_ref, nv_ref, v_ref, mix_ref, near_bias, own_bias):
        @pl.when(pl.program_id(1) == 0)
        def _():
            set_bias(sc, pl.program_id(0), near_bias, own_bias, False)

        q = q_ref[...]
        near = jnp.exp(nt(q, nk_ref[...]) + near_bias[...])
        own = jnp.exp(nt(q, k_ref[...]) + own_bias[...])
        sums = jnp.sum(near, axis=-1, keepdims=True) + jnp.sum(own, axis=-1, keepdims=True)
        mix = nn(near.astype(BF16), nv_ref[...]) + nn(own.astype(BF16), v_ref[...])
        mix_ref[...] = (mix / sums).astype(BF16)

    key_at = pl.BlockSpec((rows, HD), lambda m, h, s: (m, 0))
    value_at = pl.BlockSpec((rows, HD), lambda m, h, s: (m, 1))
    out = pl.BlockSpec((rows, HD), lambda m, h, s: (m, h))
    return call(
        body,
        (total // rows, heads),
        [out, key_at, key_at, value_at, value_at],
        [(query.shape, BF16, out)],
        [pltpu.VMEM((rows, rows), F32)] * 2,
        chain,
        scalars,
        query, near, kv, near, kv,
    )[0]


def post_attention(chain, scalars, tensor_at, x, mixed, own, part, sibling, gains, step):
    total, width = x.shape

    def body(sc, x_ref, m_ref, own_ref, part_ref, sib_ref, g_ref, br_ref, mid_ref, h_ref):
        other = joined(sc, part_ref[...], sib_ref[...])
        first, second = in_order(sc, tensor_at, own_ref[...], other)
        branch = nn(m_ref[:, :half], first) + nn(m_ref[:, half:], second)
        br_ref[...] = branch.astype(BF16)
        middle = x_ref[...].astype(F32) + branch * inv_rms(branch) * one(g_ref, ATTN_POST)
        mid_ref[...] = middle.astype(BF16)
        h_ref[...] = (middle * inv_rms(middle) * one(g_ref, FFN_IN)).astype(BF16)

    half = own.shape[0]
    wide = pl.BlockSpec((step, width), lambda i, s: (i, 0))
    shape = (total, width)
    return call(
        body,
        (total // step,),
        [wide, pl.BlockSpec((step, mixed.shape[1]), lambda i, s: (i, 0)), whole(own), whole(part), whole(sibling), whole(gains)],
        [(shape, BF16, wide)] * 3,
        [],
        chain,
        scalars,
        x, mixed, own, part, sibling, gains,
    )


def ffn_forward(chain, scalars, m, h2, wg, wu, wd, rows, tile, chunk):
    width, hidden = wg.shape
    steps = hidden // tile

    def body(sc, h_ref, wg_ref, wu_ref, wd_ref, act_ref, dact_ref, hid_ref, out_ref, acc):
        @pl.when(pl.program_id(0) == 0)
        def _():
            acc[...] = jnp.zeros_like(acc)

        w = jnp.concatenate([wg_ref[...], wu_ref[...]], 1)
        for r in range(rows // chunk):
            at = pl.ds(r * chunk, chunk)
            both = nn(h_ref[at, :], w)
            g, u = both[:, :tile], both[:, tile:]
            g2 = g * g
            t = jnp.tanh(g * (GELU_C + GELU_C * GELU_A * g2))
            half = 0.5 + 0.5 * t
            act = g * half
            dact = half + 0.5 * g * (1.0 - t * t) * (GELU_C + 3.0 * GELU_C * GELU_A * g2)
            act_ref[at, :] = act.astype(BF16)
            dact_ref[at, :] = (dact * u).astype(BF16)
            hid = (act * u).astype(BF16)
            hid_ref[at, :] = hid
            acc[at, :] += nn(hid, wd_ref[...])

        @pl.when(pl.program_id(0) == steps - 1)
        def _():
            out_ref[...] = acc[...].astype(BF16)

    col = pl.BlockSpec((width, tile), lambda i, s: (0, i))
    act = pl.BlockSpec((rows, tile), lambda i, s: (0, i))
    return call(
        body,
        (steps,),
        [pl.BlockSpec((rows, width), lambda i, s: (m, 0)), col, col, pl.BlockSpec((tile, width), lambda i, s: (i, 0))],
        [((rows, hidden), BF16, act)] * 3 + [((rows, width), BF16, pl.BlockSpec((rows, width), lambda i, s: (0, 0)))],
        [pltpu.VMEM((rows, width), F32)],
        chain,
        scalars,
        h2, wg, wu, wd,
    )


def finish_forward(chain, scalars, m, part, got, middle, cot, gain, step, output, prior):
    rows, width = part.shape
    steps = rows // step

    def body(sc, p_ref, q_ref, mid_ref, c_ref, g_ref, *refs):
        out_ref, d_ref, gain_ref = refs[-3:]

        @pl.when(pl.program_id(0) == 0)
        def _():
            begin(refs[:-3], gain_ref)

        ffn = p_ref[...].astype(F32) + q_ref[...].astype(F32)
        r3 = inv_rms(ffn)
        c = c_ref[...].astype(F32)
        n = ffn * r3
        out_ref[...] = (mid_ref[...].astype(F32) + n * one(g_ref, FFN_POST)).astype(BF16)
        d_ref[...] = pull_v(ffn, r3, one(g_ref, FFN_POST), c).astype(BF16)
        gain_ref[...] += jnp.sum(c * n, axis=0, keepdims=True)

    wide = pl.BlockSpec((step, width), lambda i, s: (i, 0))
    mine = pl.BlockSpec((step, width), lambda i, s: (m * steps + i, 0))
    return call(
        body,
        (steps,),
        [wide, wide, mine, mine, whole(gain)] + [whole(p) for p in prior],
        [
            (cot.shape, BF16, mine),
            ((rows, width), BF16, wide),
            ((1, width), F32, pl.BlockSpec((1, width), lambda i, s: (0, 0))),
        ],
        [],
        chain,
        scalars,
        part, got, middle, cot, gain, *prior,
        into={} if output is None else {0: output},
    )


def ffn_backward(chain, scalars, d_ffn, act, dact, wg, wu, wd, tile, chunk):
    width, hidden = wg.shape
    rows = d_ffn.shape[0]
    steps = hidden // tile

    def body(sc, d_ref, act_ref, dact_ref, wg_ref, wu_ref, wd_ref, dg_ref, du_ref, dh_ref, acc):
        @pl.when(pl.program_id(0) == 0)
        def _():
            acc[...] = jnp.zeros_like(acc)

        w = jnp.concatenate([wg_ref[...], wu_ref[...]], 1)
        for r in range(rows // chunk):
            at = pl.ds(r * chunk, chunk)
            dh = nt(d_ref[at, :], wd_ref[...])
            du = (dh * act_ref[at, :].astype(F32)).astype(BF16)
            dg = (dh * dact_ref[at, :].astype(F32)).astype(BF16)
            dg_ref[at, :] = dg
            du_ref[at, :] = du
            acc[at, :] += nt(jnp.concatenate([dg, du], 1), w)

        @pl.when(pl.program_id(0) == steps - 1)
        def _():
            dh_ref[...] = acc[...].astype(BF16)

    col = pl.BlockSpec((width, tile), lambda i, s: (0, i))
    acts = pl.BlockSpec((rows, tile), lambda i, s: (0, i))
    wide = pl.BlockSpec((rows, width), lambda i, s: (0, 0))
    return call(
        body,
        (steps,),
        [wide, acts, acts, col, col, pl.BlockSpec((tile, width), lambda i, s: (i, 0))],
        [((rows, hidden), BF16, acts), ((rows, hidden), BF16, acts), ((rows, width), BF16, wide)],
        [pltpu.VMEM((rows, width), F32)],
        chain,
        scalars,
        d_ffn, act, dact, wg, wu, wd,
    )


def attention_backward(chain, scalars, m, tensor_at, part, got, middle, cot, branch, gains, own, part_o, sibling_o, q, raw, head_gains,
                       cosine, sine, near, kv, prior):
    rows, width = part.shape
    per = own.shape[0] // HD
    heads = 2 * per

    def body(sc, p_ref, o_ref, mid_ref, c_ref, br_ref, g_ref, own_ref, part_ref, sib_ref, q_ref, raw_ref, gq_ref,
             cos_ref, sin_ref, nk_ref, k_ref, nv_ref, v_ref, *refs):
        (dm_ref, db_ref, dq_ref, dn_ref, dk_ref, dv_ref, sum_f_ref, sum_a_ref, sum_q_ref,
         near_bias, own_bias, near_kt, own_kt, acc) = refs[len(prior):]
        h = pl.program_id(0)

        @pl.when(h == 0)
        def _():
            set_bias(sc, m, near_bias, own_bias, True)
            near_kt[...] = nk_ref[...].T
            own_kt[...] = k_ref[...].T
            acc[...] = jnp.zeros_like(acc)
            begin(refs[:len(prior)], sum_f_ref, sum_a_ref, sum_q_ref)
            for r in range(rows // 128):
                at = pl.ds(r * 128, 128)
                e = p_ref[at, :].astype(F32) + o_ref[at, :].astype(F32)
                mid = mid_ref[at, :].astype(F32)
                r2 = inv_rms(mid)
                d_mid = c_ref[at, :].astype(F32) + pull_v(mid, r2, one(g_ref, FFN_IN), e)
                dm_ref[at, :] = d_mid.astype(BF16)
                sum_f_ref[...] += jnp.sum(e * mid * r2, axis=0, keepdims=True)
                branch = br_ref[at, :].astype(F32)
                r1 = inv_rms(branch)
                sum_a_ref[...] += jnp.sum(d_mid * branch * r1, axis=0, keepdims=True)
                db_ref[at, :] = pull_v(branch, r1, one(g_ref, ATTN_POST), d_mid).astype(BF16)

        other = jnp.where(h % per == sc[1], part_ref[...], sib_ref[...])
        wo = jnp.where(h // per == sc[tensor_at], own_ref[...], other)
        d_mix = nt(db_ref[...], wo).astype(BF16)
        qv = q_ref[...]
        near = jnp.exp(nt(nk_ref[...], qv) + near_bias[...])
        own = jnp.exp(nt(k_ref[...], qv) + own_bias[...])
        inv = 1.0 / (jnp.sum(near, axis=0, keepdims=True) + jnp.sum(own, axis=0, keepdims=True))
        near = near * inv
        own = own * inv
        acc[2] += nn(near.astype(BF16), d_mix)
        acc[3] += nn(own.astype(BF16), d_mix)
        dp_near = nt(nv_ref[...], d_mix)
        dp_own = nt(v_ref[...], d_mix)
        dots = jnp.sum(near * dp_near, axis=0, keepdims=True) + jnp.sum(own * dp_own, axis=0, keepdims=True)
        ds_near = (near * (dp_near - dots)).astype(BF16)
        ds_own = (own * (dp_own - dots)).astype(BF16)
        acc[0] += nn(ds_near, qv)
        acc[1] += nn(ds_own, qv)
        d_q = (nn(near_kt[...], ds_near) + nn(own_kt[...], ds_own)).T
        e_q = rotate_back(d_q * SCALE, cos_ref[...], sin_ref[...])
        raw_v = raw_ref[...].astype(F32)
        rq = inv_rms(raw_v)
        sum_q_ref[...] += jnp.sum(e_q * raw_v * rq, axis=0, keepdims=True)
        dq_ref[...] = pull_v(raw_v, rq, one(gq_ref, QUERY), e_q).astype(BF16)

        @pl.when(h == heads - 1)
        def _():
            dn_ref[:, :HD] = acc[0].astype(BF16)
            dk_ref[...] = acc[1]
            dn_ref[:, HD:] = acc[2].astype(BF16)
            dv_ref[...] = acc[3]

    wide = pl.BlockSpec((rows, width), lambda h, s: (0, 0))
    mine = pl.BlockSpec((rows, width), lambda h, s: (m, 0))
    key_at = pl.BlockSpec((rows, HD), lambda h, s: (m, 0))
    value_at = pl.BlockSpec((rows, HD), lambda h, s: (m, 1))
    heads_at = pl.BlockSpec((rows, HD), lambda h, s: (m, h))
    small = pl.BlockSpec((rows, HD), lambda h, s: (0, 0))
    sums = pl.BlockSpec((1, width), lambda h, s: (0, 0))
    weight = pl.BlockSpec((HD, width), lambda h, s: (h % per, 0))
    return call(
        body,
        (heads,),
        [wide, wide, mine, mine, mine, whole(gains), weight, whole(part_o), whole(sibling_o), heads_at, heads_at, whole(head_gains), whole(cosine), whole(sine),
         key_at, key_at, value_at, value_at] + [whole(p) for p in prior],
        [
            ((rows, width), BF16, wide),
            ((rows, width), BF16, wide),
            ((rows, heads * HD), BF16, pl.BlockSpec((rows, HD), lambda h, s: (0, h))),
            ((rows, 2 * HD), BF16, pl.BlockSpec((rows, 2 * HD), lambda h, s: (0, 0))),
            ((rows, HD), F32, small),
            ((rows, HD), F32, small),
            ((1, width), F32, sums),
            ((1, width), F32, sums),
            ((1, HD), F32, pl.BlockSpec((1, HD), lambda h, s: (0, 0))),
        ],
        [pltpu.VMEM((rows, rows), F32)] * 2 + [pltpu.VMEM((HD, rows), BF16)] * 2 + [pltpu.VMEM((4, rows, HD), F32)],
        chain,
        scalars,
        part, got, middle, cot, branch, gains, own, part_o, sibling_o, q, raw, head_gains, cosine, sine,
        near, kv, near, kv, *prior,
    )


def input_gradient(chain, scalars, m, tensor_at, x, d_mid, dq, dk, dv, got, raw, head_gains, cosine, sine, wq, wk, wv, gains, step, grad, prior):
    rows, width = d_mid.shape
    steps = rows // step

    def body(sc, x_ref, dm_ref, dq_ref, dk_ref, dv_ref, gk_ref, gv_ref, raw_ref, g_ref, cos_ref, sin_ref,
             own_ref, part_ref, sib_ref, wk_ref, wv_ref, gain_ref, *refs):
        out_ref, kv_ref, sum_ref, sum_k_ref = refs[-4:]

        @pl.when(pl.program_id(0) == 0)
        def _():
            begin(refs[:-4], sum_ref, sum_k_ref)

        e = rotate_back(dk_ref[...] + gk_ref[...].astype(F32), cos_ref[...], sin_ref[...])
        raw_v = raw_ref[...]
        rk = inv_rms(raw_v)
        sum_k_ref[...] += jnp.sum(e * raw_v * rk, axis=0, keepdims=True)
        dkr = pull_v(raw_v, rk, one(g_ref, KEY), e).astype(BF16)
        dvr = (dv_ref[...] + gv_ref[...].astype(F32)).astype(BF16)
        kv_ref[:, :HD] = dkr
        kv_ref[:, HD:] = dvr
        other = joined(sc, part_ref[...], sib_ref[...])
        first, second = in_order(sc, tensor_at, own_ref[...], other)
        half = first.shape[1]
        d_h = nt(dq_ref[:, :half], first) + nt(dq_ref[:, half:], second) + nt(dkr, wk_ref[...]) + nt(dvr, wv_ref[...])
        v = x_ref[...].astype(F32)
        r0 = inv_rms(v)
        sum_ref[...] += jnp.sum(d_h * v * r0, axis=0, keepdims=True)
        out_ref[...] = dm_ref[...].astype(F32) + pull_v(v, r0, one(gain_ref, ATTN_IN), d_h)

    wide = pl.BlockSpec((step, width), lambda i, s: (i, 0))
    mine = pl.BlockSpec((step, width), lambda i, s: (m * steps + i, 0))
    head = pl.BlockSpec((step, HD), lambda i, s: (i, 0))
    table = pl.BlockSpec((step, HD // 2), lambda i, s: (i, 0))
    return call(
        body,
        (steps,),
        [mine, wide, pl.BlockSpec((step, dq.shape[1]), lambda i, s: (i, 0)), head, head, head,
         pl.BlockSpec((step, HD), lambda i, s: (i, 1)),
         pl.BlockSpec((step, HD), lambda i, s: (m * steps + i, 0)), whole(head_gains), table, table,
         *[whole(w) for w in wq], whole(wk), whole(wv), whole(gains), *[whole(p) for p in prior]],
        [
            (x.shape, F32, mine),
            ((rows, 2 * HD), BF16, pl.BlockSpec((step, 2 * HD), lambda i, s: (i, 0))),
            ((1, width), F32, pl.BlockSpec((1, width), lambda i, s: (0, 0))),
            ((1, HD), F32, pl.BlockSpec((1, HD), lambda i, s: (0, 0))),
        ],
        [],
        chain,
        scalars,
        x, d_mid, dq, dk, dv, got, got, raw, head_gains, cosine, sine, *wq, wk, wv, gains, *prior,
        into={} if grad is None else {0: grad},
    )


def weight_gradient(chain, scalars, lefts, rights, n, tile, tiles, chunk, right_at, out_at, out_tiles, into=None, extra=None):
    width = lefts[0][0].shape[1]
    rows = WINDOW
    rps = width // n
    count = len(lefts)

    def body(sc, *refs):
        l_refs, r_refs = refs[:count], refs[count:2 * count]
        send_ref, keep_ref, left_t = refs[-3:]

        @pl.when(pl.program_id(0) == 0)
        def _():
            for k in range(count):
                left_t[:, k * rows:(k + 1) * rows] = l_refs[k][...].T

        even = sc[1] == 0
        if extra is not None:
            filled = jnp.zeros((128 - extra.shape[0], width), F32)
            more_t = jnp.concatenate([refs[2 * count][...], filled], 0).T
        for c in range(width // chunk):
            v = nn(left_t[c * chunk:(c + 1) * chunk, :rows], r_refs[0][...])
            for k in range(1, count):
                v += nn(left_t[c * chunk:(c + 1) * chunk, k * rows:(k + 1) * rows], r_refs[k][...])
            if extra is not None:
                v = jnp.concatenate([v, more_t[c * chunk:(c + 1) * chunk]], 1)
            for j in range(chunk // (2 * rps)):
                a = v[2 * j * rps:(2 * j + 1) * rps]
                b = v[(2 * j + 1) * rps:(2 * j + 2) * rps]
                at = c * (chunk // (2 * rps)) + j
                send_ref[at] = jnp.where(even, b, a).astype(BF16)
                keep_ref[at] = jnp.where(even, a, b).astype(BF16)

    more = 0 if extra is None else 128
    out = pl.BlockSpec((n // 2, rps, tile + more), lambda i, s: (0, 0, out_at + i))
    shape = (n // 2, rps, out_tiles * tile + more)

    def left_spec(at):
        return pl.BlockSpec((rows, width), lambda i, s: (at, 0))

    def right_spec(at):
        return pl.BlockSpec((rows, tile), lambda i, s: (at, right_at(s) + i))

    return call(
        body,
        (tiles,),
        [left_spec(at) for _, at in lefts] + [right_spec(at) for _, at in rights]
        + ([] if extra is None else [whole(extra)]),
        [(shape, BF16, out), (shape, BF16, out)],
        [pltpu.VMEM((width, count * rows), BF16)],
        chain,
        scalars,
        *[l for l, _ in lefts], *[r for r, _ in rights], *([] if extra is None else [extra]),
        into=None if into is None else {0: into[0], 1: into[1]},
    )


def plain_gradient(lefts, rights, n, tile, tiles, start, extra=None):
    width = lefts[0][0].shape[1]
    total = 0.0
    for (left, la), (right, ra) in zip(lefts, rights):
        left = left[la * WINDOW:(la + 1) * WINDOW]
        right = lax.dynamic_slice_in_dim(right[ra * WINDOW:(ra + 1) * WINDOW], start * tile, tile * tiles, 1)
        total = total + lax.dot_general(left, right, (((0,), (0,)), ((), ())), preferred_element_type=F32)
    if extra is not None:
        total = jnp.concatenate([total, jnp.pad(extra.T, ((0, 0), (0, 120)))], 1)
    both = total.astype(BF16).reshape(n // 2, 2, width // n, -1)
    core = my_bit(0)
    return (
        lax.dynamic_index_in_dim(both, 1 - core, 1, keepdims=False),
        lax.dynamic_index_in_dim(both, core, 1, keepdims=False),
    )


class Halving:
    def __init__(self, chain, at, send, keep, order):
        self.chain = chain
        self.at = at
        self.sum = None
        self.bits = list(range(1, lax.axis_size("dp").bit_length() - 1))[::-1]
        self.order = list(order)
        shape = (2,) * len(self.bits) + keep.shape[1:]
        self.parts = [(keep.reshape(shape), self.bits), (chain.moved(swap_dp(send, 0)).reshape(shape), self.bits)]

    def job(self):
        bit = self.order.pop(0) if self.order else None
        self.bits = [b for b in self.bits if b != bit]
        rps, columns = self.parts[0][0].shape[-2:]
        bits, at = self.bits if bit is not None else [], self.at

        def block_at(p_bits, tile):
            def index(j, s):
                def value(b):
                    mine = (s[at] >> b) & 1
                    return 1 - mine if b == bit else mine

                return tuple(0 if b in bits else value(b) for b in p_bits) + (0, j)

            return pl.BlockSpec(tuple(2 if b in bits else None for b in p_bits) + (rps, tile), index)

        def done(out):
            if bit is None:
                self.sum = out
            else:
                self.parts.append((self.chain.moved(swap_dp(out, bit)), bits))

        dtype = F32 if bit is None else BF16
        shape = (2,) * len(bits) + (rps, columns)
        return self.parts[:], block_at, shape, dtype, done


def add_parts(chain, scalars, *halvings, handed=None):
    jobs = [h.job() for h in halvings]
    steps = 1 if all(j[2][-1] % 384 == 0 for j in jobs) else 1
    ins, outs, args = [], [], []
    for parts, block_at, shape, dtype, _ in jobs:
        tile = shape[-1] // steps
        lead = shape[:-2]
        args += [p for p, _ in parts]
        ins += [block_at(bits, tile) for _, bits in parts]
        spec = pl.BlockSpec(shape[:-1] + (tile,), lambda j, s, z=(0,) * (len(lead) + 1): z + (j,))
        outs.append((shape, dtype, spec))

    more = {}
    if handed is not None:
        outs.insert(0, (handed.shape, handed.dtype, pl.BlockSpec(memory_space=pl.ANY)))
        more = dict(into={0: handed}, ahead=chain.received)

    def body(sc, *refs):
        left = refs[:len(args)]
        for (parts, _, _, dtype, _), out in zip(jobs, refs[len(refs) - len(jobs):]):
            total = left[0][...].astype(F32)
            for r in left[1:len(parts)]:
                total += r[...].astype(F32)
            out[...] = total.astype(dtype)
            left = left[len(parts):]

    results = call(body, (steps,), ins, outs, [], chain, scalars, *args, **more)
    if handed is not None:
        handed, *results = results
    for (_, _, _, _, done), out in zip(jobs, results):
        done(out)
    return handed


def shards(
    tokens,
    image_starts,
    g_attn_in,
    w_query,
    w_key,
    w_value,
    g_query,
    g_key,
    w_out,
    g_attn_post,
    g_ffn_in,
    w_gate,
    w_up,
    w_down,
    g_ffn_post,
    cotangent,
):
    mb, rows, width = tokens.shape
    own = w_query.shape[1]
    y = lax.axis_index("tensor")
    dp = lax.axis_index("dp")
    n = lax.axis_size("dp")
    offset = dp % (SEQ_LEN // rows) * rows
    cosine, sine = angle_tables(offset + jnp.arange(rows, dtype=jnp.int32))
    core = my_bit(0)
    scalars = jnp.concatenate([jnp.stack([offset, core]), image_starts[:, 0], jnp.stack([y, dp])]).astype(jnp.int32)
    low_first = list(range(1, n.bit_length() - 1))
    low_last = low_first[1:] + low_first[:1]

    x = tokens.reshape(mb * rows, width)
    cot = cotangent.reshape(mb * rows, width)
    chain = Chain()

    gains = jnp.stack([g_attn_in, g_attn_post, g_ffn_in, g_ffn_post])
    head_gains = jnp.stack([g_query, g_key])
    tensor_at = 2 + mb
    part_q = chain.moved(swap_y(pick(w_query.reshape(2, width // 2, own), core)))
    h1, key_raw, kv = pre_attention(
        chain, scalars, x, gains, w_key, w_value, head_gains, cosine, sine, rows
    )
    near = chain.moved(shift_dp(kv, 1))
    sibling_q = chain.moved(swap_dp(after(part_q, kv), 0))
    part_o = chain.moved(swap_y(pick(after(w_out, part_q).reshape(2, own // 2, width), core)))
    pair = None
    for other in (None, (part_q, sibling_q)):
        pair = queries(
            chain, scalars, tensor_at, h1, w_query, other, head_gains, cosine, sine, rows, pair
        )
    query_raw, query = pair
    mixed = attention(chain, scalars, query, near, kv, rows)
    sibling_o = chain.moved(swap_dp(after(part_o, mixed), 0))
    other_o = (part_o, sibling_o)
    branch, middle, h2 = post_attention(
        chain, scalars, tensor_at, x, mixed, w_out, *other_o, gains, rows
    )

    forward = []
    for m in range(mb):
        act, dact, hidden, part = ffn_forward(chain, scalars, m, h2, w_gate, w_up, w_down, rows, 1152, 256)
        forward.append((act, dact, hidden, part, chain.moved(swap_y(part))))

    split = width // n % 8 == 0
    hidden_width = w_gate.shape[1]

    def gradient(lefts, rights, tile, tiles, first=0, own_tile=False, out_at=0, out_tiles=None, into=None, extra=None):
        if split:
            right_at = (lambda s: s[tensor_at]) if own_tile else (lambda s: first)
            return weight_gradient(
                chain, scalars, lefts, rights, n, tile, tiles, 576, right_at, out_at, out_tiles or tiles, into, extra
            )
        made = plain_gradient(lefts, rights, n, tile, tiles, y if own_tile else first, extra)
        if into is None:
            return made
        return tuple(jnp.concatenate(p, -1) for p in zip(into, made))

    def batches(a):
        return [(a, m) for m in range(mb)]

    def each(arrays):
        return [(a, 0) for a in arrays]

    def halving(pair, order):
        return Halving(chain, 3 + mb, *pair, order)

    def serve(*halvings, handed=None):
        for h in halvings[:-1]:
            add_parts(chain, scalars, h)
        return add_parts(chain, scalars, halvings[-1], handed=handed)

    output = None
    d_ffns, grads, parts = [], [], []
    post_sum = ()
    hiddens = each([f[2] for f in forward])
    for m in range(mb):
        act, dact, hidden, part, got = forward[m]
        output, d_ffn, *post_sum = finish_forward(
            chain, scalars, m, part, got, middle, cot, gains, rows // 2, output, post_sum
        )
        d_ffns.append(d_ffn)
        if m == mb - 1:
            down = halving(gradient(each(d_ffns), hiddens, 1152, 3), low_last)
        d_gate, d_up, dh = ffn_backward(chain, scalars, d_ffn, act, dact, w_gate, w_up, w_down, 1152, 512)
        grads.append((d_gate, d_up))
        parts.append((dh, chain.moved(swap_y(dh))))

    serve(down)
    gate = halving(gradient(batches(h2), each([g[0] for g in grads]), 1152, 3), low_first)
    up = halving(gradient(batches(h2), each([g[1] for g in grads]), 1152, 3), low_first)
    serve(gate)
    chain.before_next(parts[1][1])

    back = []
    shifted = []
    for m in range(mb):
        back.append(
            attention_backward(
                chain, scalars, m, tensor_at, *parts[m], middle, cot, branch, gains, w_out, *other_o, query,
                query_raw, head_gains, cosine, sine, near, kv, back[-1][6:] if back else (),
            )
        )
        shifted.append(chain.moved(shift_dp(back[m][3], -1)))
        if m == 0:
            serve(down)
    serve(up)
    chain.before_next(shifted[0])
    own_at = dict(own_tile=True, out_tiles=2)
    pair = gradient(each([b[1] for b in back]), batches(mixed), own, 1, **own_at)
    pair = gradient(batches(h1), each([b[2] for b in back]), own, 1, out_at=1, into=pair, **own_at)
    attn = halving(pair, low_first)
    serve(gate)

    grad_input = None
    kvs = []
    in_sums = ()
    for m in range(mb):
        d_mid, d_branch, dq, _, dk, dv = back[m][:6]
        grad_input, dkv, *in_sums = input_gradient(
            chain, scalars, m, tensor_at, x, d_mid, dq, dk, dv, shifted[m], key_raw, head_gains, cosine, sine,
            (w_query, part_q, sibling_q), w_key, w_value, gains, rows // 2, grad_input, in_sums,
        )
        kvs.append(dkv)
        if m == 0:
            serve(down, attn, gate, up)

    rps = width // n
    hps = HD // n

    def spread(sums):
        return jnp.pad(sums.reshape(n, hps), ((0, 0), (0, rps - hps))).reshape(1, width)

    extra = jnp.concatenate(
        [
            in_sums[0],
            post_sum[0],
            back[-1][6],
            back[-1][7],
            spread(back[-1][8]),
            spread(in_sums[1]),
            jnp.zeros((2, width), F32),
        ]
    )
    last = halving(gradient(batches(h1), each(kvs), 2 * HD, 1, extra=extra), low_first)
    serve(attn, last, up, down, last, attn, gate, last)
    every = (attn, down, gate, up, last)
    while last.order:
        serve(*[h for h in every if h.order])
    output = serve(*[h for h in every if h.sum is None], handed=output)
    last, grad_attn = last.sum, attn.sum
    gain_grads = last[:, 2 * HD:]
    return (
        output.reshape(tokens.shape),
        grad_input.reshape(tokens.shape),
        gain_grads[:, 0],
        grad_attn[:, own:],
        last[:, :HD],
        last[:, HD:2 * HD],
        gain_grads[:hps, 4],
        gain_grads[:hps, 5],
        grad_attn[:, :own].T,
        gain_grads[:, 3],
        gain_grads[:, 2],
        gate.sum,
        up.sum,
        down.sum.T,
        gain_grads[:, 1],
    )


def solution(mesh):
    rows = P(None, "dp", None)
    in_specs = (
        rows,
        P(None, "dp"),
        P(),
        P(None, "tensor"),
        P(),
        P(),
        P(),
        P(),
        P("tensor", None),
        P(),
        P(),
        P(None, "tensor"),
        P(None, "tensor"),
        P("tensor", None),
        P(),
        rows,
    )
    out_specs = (
        rows,
        rows,
        P("dp"),
        P("dp", "tensor"),
        P("dp", None),
        P("dp", None),
        P("dp"),
        P("dp"),
        P("tensor", "dp"),
        P("dp"),
        P("dp"),
        P("dp", "tensor"),
        P("dp", "tensor"),
        P("tensor", "dp"),
        P("dp"),
    )
    return jax.shard_map(shards, mesh=mesh, in_specs=in_specs, out_specs=out_specs, check_vma=False)
```
